256 devices in a mesh: row: 64 (over x, z, core), col: 4 (over y).
Axes of the slice: x: 4, y: 4, z: 8, core: 2. Of those that a mesh axis runs over, the one named last changes fastest.
Arguments:
- krylov: float32 [8, 1024, 256], P(None, 'row'), may hold values from -8 to 8
- self_weight: float32 [1024, 256], P('row'), may hold values from 0.5 to 2
- cluster_basis: bfloat16 [1024, 64, 256], P('row'), may hold values from -0.375 to 0.375
- transfer: float32 [1024, 64, 64], P('row'), may hold values from -0.75 to 0.75
- near_blocks: bfloat16 [1024, 8, 256, 256], P('row', 'col'), may hold values from -0.125 to 0.125
- near_cols: int32 [1024, 8], P('row', 'col'), may hold values from 0 to 1023, as said below
- far_row: int32 [64, 4, 64], P('row', 'col'), may hold values from 0 to 1023, as said below
- far_col: int32 [64, 4, 64], P('row', 'col'), may hold values from 0 to 1023, as said below
- far_mat: float32 [64, 4, 64, 64, 64], P('row', 'col'), may hold values from -0.1875 to 0.1875
- coarse_row: int32 [64, 4, 16], P('row', 'col'), may hold values from 0 to 255, as said below
- coarse_col: int32 [64, 4, 16], P('row', 'col'), may hold values from 0 to 255, as said below
- coarse_mat: float32 [64, 4, 16, 64, 64], P('row', 'col'), may hold values from -0.1875 to 0.1875
Outputs:
- new_vectors: float32 [2, 1024, 256], P(None, 'row')
- hessen: float32 [2, 10], replicated
The draws below stay inside these ranges and needn't reach their ends.
Inputs may be any that keep to these rules, and one draw needn't show every extreme that they name: `near_cols`: each near-field column leaf lies within 16 leaves of its row leaf, counted cyclically over 1024; both ends of that reach occur. `far_row`: blocks at row index r have row leaves r * 16 to (r + 1) * 16 - 1. `far_col`: blocks in column group c have column leaves equal to c modulo 4. `coarse_row`: blocks at row index r have row parents r * 4 to (r + 1) * 4 - 1. `coarse_col`: blocks in column group c have column parents equal to c modulo 4.
All inputs are finite; a program needn't handle non-finite values.
Results may differ from the reference program's by a relative error of at most 0.0025.
Values may be sent and summed in bfloat16 or wider, within the bound.
A program may use at most 64 MiB of HBM per device.

```python
import math
import jax
import jax.numpy as jnp
from jax import lax

P_SIZE = 256
R = 64
LEAF_DEV = 16
CHILD = 4
FAR_LEAF = 16
CFAR_PAR = 16
KRY = 8
LEAVES = 1024
PAR_DEV = 4
PARENTS = 256
NEAR_LEAF = 8
FAR_DEV = 64
CFAR_DEV = 16
N_ROW = 64
N_COL = 4


def draw_krylov(key, part):
    key = jax.random.fold_in(key, 7)
    first, second = jax.random.split(key, 2)
    common = jax.random.normal(first, (LEAVES, P_SIZE), jnp.float32)
    own = jax.random.normal(second, (KRY, LEAVES, P_SIZE), jnp.float32)
    values = own + 0.6 * common
    return jnp.clip(values, -8.0, 8.0)


def draw_near_cols(key, part):
    key = jax.random.fold_in(key, 11)
    first, second, third = jax.random.split(key, 3)
    offsets = jax.random.randint(first, (LEAVES, NEAR_LEAF), -LEAF_DEV, LEAF_DEV + 1)
    upper = jax.random.randint(second, (), 0, LEAVES)
    lower = jax.random.randint(third, (), 0, LEAVES)
    offsets = offsets.at[upper, 0].set(LEAF_DEV)
    offsets = offsets.at[lower, NEAR_LEAF - 1].set(-LEAF_DEV)
    return ((jnp.arange(LEAVES, dtype=jnp.int32)[:, None] + offsets + LEAVES) % LEAVES).astype(jnp.int32)


def draw_far_row(key, part):
    key = jax.random.fold_in(key, 13)
    base = jnp.arange(N_ROW, dtype=jnp.int32)[:, None, None] * LEAF_DEV
    return (base + jax.random.randint(key, (N_ROW, N_COL, FAR_DEV), 0, LEAF_DEV)).astype(jnp.int32)


def draw_far_col(key, part):
    key = jax.random.fold_in(key, 17)
    group = jnp.arange(N_COL, dtype=jnp.int32)[None, :, None]
    picks = jax.random.randint(key, (N_ROW, N_COL, FAR_DEV), 0, LEAVES // N_COL)
    return (picks * N_COL + group).astype(jnp.int32)


def draw_coarse_row(key, part):
    key = jax.random.fold_in(key, 19)
    base = jnp.arange(N_ROW, dtype=jnp.int32)[:, None, None] * PAR_DEV
    return (base + jax.random.randint(key, (N_ROW, N_COL, CFAR_DEV), 0, PAR_DEV)).astype(jnp.int32)


def draw_coarse_col(key, part):
    key = jax.random.fold_in(key, 23)
    group = jnp.arange(N_COL, dtype=jnp.int32)[None, :, None]
    picks = jax.random.randint(key, (N_ROW, N_COL, CFAR_DEV), 0, PARENTS // N_COL)
    return (picks * N_COL + group).astype(jnp.int32)


def block_scale(stream_key, extent, pieces, low, high):
    def one(axis_at, shards_of):
        steps = jax.random.uniform(jax.random.fold_in(jax.random.fold_in(stream_key, 6), axis_at), (shards_of,), jnp.float32, low / len(pieces), high / len(pieces))
        return jnp.repeat(jnp.exp(steps), extent[axis_at] // shards_of).reshape((-1,) + (1,) * (len(extent) - axis_at - 1))

    level = one(*pieces[0])
    for cut in pieces[1:]:
        level = level * one(*cut)
    return level


def noise(rng, dims, spread, most, pieces=(), held_as=jnp.bfloat16):
    factor_of = block_scale(rng, dims, pieces, -0.22, 0.18) if pieces else 1.0
    drawn = jax.random.normal(rng, dims, jnp.float32) * spread * factor_of
    return jnp.minimum(jnp.maximum(drawn, -most), most).astype(held_as)


def setup_inputs(seed: int = 0) -> dict:
    seeds = jax.random.split(jax.random.key(seed), 13)
    krylov = draw_krylov(jax.random.fold_in(seeds[12], 71), 0)
    self_weight = jnp.clip(jnp.exp(math.log(2.0) - 1.3862944 * jax.random.uniform(seeds[1], (LEAVES, P_SIZE), jnp.float32) ** block_scale(seeds[1], (LEAVES, P_SIZE), ((0, 64),), -0.2, 0.2)), 0.5, 2.0)
    cluster_basis = noise(seeds[2], (LEAVES, R, P_SIZE), P_SIZE ** -0.5, 0.375, ((0, 64),))
    transfer = noise(seeds[3], (LEAVES, R, R), R ** -0.5, 0.75, ((0, 64),), jnp.float32)
    near_blocks = noise(seeds[4], (LEAVES, NEAR_LEAF, P_SIZE, P_SIZE), (P_SIZE * NEAR_LEAF) ** -0.5, 0.125, ((0, 64), (1, 4)))
    near_cols = draw_near_cols(jax.random.fold_in(seeds[12], 71), 0)
    far_row = draw_far_row(jax.random.fold_in(seeds[12], 71), 0)
    far_col = draw_far_col(jax.random.fold_in(seeds[12], 71), 0)
    far_mat = noise(seeds[8], (N_ROW, N_COL, FAR_DEV, R, R), (R * FAR_LEAF) ** -0.5, 0.1875, ((0, 64), (1, 4)), jnp.float32)
    coarse_row = draw_coarse_row(jax.random.fold_in(seeds[12], 71), 0)
    coarse_col = draw_coarse_col(jax.random.fold_in(seeds[12], 71), 0)
    coarse_mat = noise(seeds[11], (N_ROW, N_COL, CFAR_DEV, R, R), (R * CFAR_PAR) ** -0.5, 0.1875, ((0, 64), (1, 4)), jnp.float32)
    return dict(krylov=krylov, self_weight=self_weight, cluster_basis=cluster_basis, transfer=transfer, near_blocks=near_blocks, near_cols=near_cols, far_row=far_row, far_col=far_col, far_mat=far_mat, coarse_row=coarse_row, coarse_col=coarse_col, coarse_mat=coarse_mat)


HIGH = lax.Precision.HIGHEST

def apply_operator(v, self_weight, cluster_basis, transfer, near_blocks, near_cols, far_row, far_col, far_mat, coarse_row, coarse_col, coarse_mat):
    vb = v.astype(jnp.bfloat16)
    basis_wide = cluster_basis.astype(jnp.float32)
    coef = jnp.einsum('jap,jp->ja', basis_wide, vb.astype(jnp.float32), precision=HIGH)
    lifted = jnp.einsum('kab,ka->kb', transfer, coef, precision=HIGH)
    pcoef = lifted.reshape(PARENTS, CHILD, R).sum(axis=1)

    def near_leaf(items):
        blocks, cols = items
        picked = vb[cols].astype(jnp.float32)
        return jnp.einsum('spq,sq->p', blocks.astype(jnp.float32), picked, precision=HIGH)
    near = lax.map(near_leaf, (near_blocks, near_cols))
    rows_flat = far_row.reshape(-1)
    cols_flat = far_col.reshape(-1)
    contrib = jnp.einsum('bac,bc->ba', far_mat.reshape(-1, R, R), coef[cols_flat], precision=HIGH)
    far = jnp.zeros((LEAVES, R), jnp.float32).at[rows_flat].add(contrib)
    crow = coarse_row.reshape(-1)
    ccol = coarse_col.reshape(-1)
    ccontrib = jnp.einsum('bac,bc->ba', coarse_mat.reshape(-1, R, R), pcoef[ccol], precision=HIGH)
    cres = jnp.zeros((PARENTS, R), jnp.float32).at[crow].add(ccontrib)
    down = jnp.einsum('kab,kb->ka', transfer, jnp.repeat(cres, CHILD, axis=0), precision=HIGH)
    farb = (far + down).astype(jnp.bfloat16)
    back = jnp.einsum('jap,ja->jp', basis_wide, farb.astype(jnp.float32), precision=HIGH)
    return self_weight * v + near + back

def reference(krylov, self_weight, cluster_basis, transfer, near_blocks, near_cols, far_row, far_col, far_mat, coarse_row, coarse_col, coarse_mat):
    count = float(LEAVES * P_SIZE)
    vectors = krylov
    current = krylov[KRY - 1]
    outputs = []
    columns = []
    for step in range(2):
        w = apply_operator(current, self_weight, cluster_basis, transfer, near_blocks, near_cols, far_row, far_col, far_mat, coarse_row, coarse_col, coarse_mat)
        proj = jnp.einsum('kip,ip->k', vectors, w, precision=HIGH) / count
        w2 = w - jnp.einsum('k,kip->ip', proj, vectors, precision=HIGH)
        beta = jnp.sqrt(jnp.sum(w2 * w2) / count + 1e-06)
        current = w2 / beta
        outputs.append(current)
        vectors = jnp.concatenate([vectors, current[None]], axis=0)
        if step == 0:
            columns.append(jnp.concatenate([proj, jnp.zeros((1,), jnp.float32), beta[None]]))
        else:
            columns.append(jnp.concatenate([proj, beta[None]]))
    return (jnp.stack(outputs), jnp.stack(columns))
```

```python
import functools

import jax
import jax.numpy as jnp
from jax import lax
from jax.experimental import pallas as pl
from jax.experimental.pallas import tpu as pltpu
from jax.sharding import PartitionSpec as P

MESH = pl.DeviceIdType.MESH
F32 = jnp.float32
BF16 = jnp.bfloat16

NX, NZ, NCORE, NCOL = 4, 8, 2, 4
NROW = NX * NZ * NCORE
LEAF, PANEL, RANK, KRY = 16, 256, 64, 8
LEAVES = NROW * LEAF
FAR, COARSE = 64, 16
COUNT = float(LEAVES * PANEL)


def iota(shape, dim):
    return lax.broadcasted_iota(jnp.int32, shape, dim)


def nt(a, b):
    return lax.dot_general(a, b, (((1,), (1,)), ((), ())), preferred_element_type=F32)


def split(x):
    hi = x.astype(BF16)
    return hi, (x - hi.astype(F32)).astype(BF16)


def fold(x):
    s = x[:, :128] + x[:, 128:]
    return s + pltpu.roll(s, 64, 1)


def partial_sum(x):
    s = x[:8] + x[8:]
    return jnp.sum(s[:, :128] + s[:, 128:], axis=0, keepdims=True)


def lanes_of(rows, first):
    sums = jnp.sum(rows, axis=1, keepdims=True)
    n = rows.shape[0]
    return jnp.sum(jnp.where(iota((n, 128), 1) == iota((n, 128), 0) + first, sums, 0.0), axis=0, keepdims=True)


def stack_rows(rows, n):
    out = jnp.zeros((n, 128), F32)
    at = iota((n, 128), 0)
    for j, r in enumerate(rows):
        out = jnp.where(at == j, r, out)
    return out


def kernel(
    kry_h, sw_h, cb_h, tr_h, nb_h, fm_h, cm_h, nc_h, fr_h, fc_h, cr_h, cc_h,
    out_v, out_h,
    nc_s, fr_s, fc_s, cr_s, cc_s,
    kry, sw, cb, bfar, tr, nb, fm, cm,
    pb, ftile, ttile, fmask, fpar, gram_rows,
    pay, tab, halo_src, halo, vpad, grow, near_src, near_tab, far_src, far_tab, sc_src, sc_tab,
    load_sem, pay_s, pay_r, halo_s, halo_r, near_s, near_r, far_s, far_r, sc_s, sc_r,
):
    me = lax.axis_index("row")
    col = lax.axis_index("col")
    x = me // (NZ * NCORE)
    z = lax.rem(me // NCORE, NZ)
    core = lax.rem(me, NCORE)
    start = me * LEAF

    loads = []

    def load(src, dst):
        c = pltpu.make_async_copy(src, dst, load_sem.at[len(loads)])
        c.start()
        loads.append(c)
        return c

    l_kry = load(kry_h, kry)
    l_cb = load(cb_h, cb)
    l_bf = [load(cb_h.at[4 * k + col], bfar.at[k]) for k in range(4)]
    l_tr = load(tr_h, tr)
    l_fm = load(fm_h, fm)
    l_cm = load(cm_h, cm)
    l_nb = load(nb_h, nb)
    l_sw = load(sw_h, sw)
    l_index = [load(h, s) for h, s in ((nc_h, nc_s), (fr_h, fr_s), (fc_h, fc_s), (cr_h, cr_s), (cc_h, cc_s))]

    bar = pltpu.get_barrier_semaphore()

    def far_peer(k):
        jz = k // (NX * NCORE)
        rest = lax.rem(k, NX * NCORE)
        jx = rest // NCORE
        jc = lax.rem(rest, NCORE)
        dz = NZ // 2 + (1 - 2 * lax.rem(jz, 2)) * ((jz + 1) // 2) + NZ
        dx = NX // 2 + (1 - 2 * lax.rem(jx, 2)) * ((jx + 1) // 2) + NX
        pz = lax.rem(z + dz, NZ)
        px = lax.rem(x + dx, NX)
        pc = lax.rem(core + 1 + jc, NCORE)
        return (px * NZ + pz) * NCORE + pc

    def to_row(body):
        def step(k, c):
            body(far_peer(k))
            return c
        lax.fori_loop(0, NROW - 1, step, 0, unroll=7)

    to_row(lambda p: pl.semaphore_signal(bar, inc=1, device_id=(p, col), device_id_type=MESH))
    for k in range(1, NCOL):
        pl.semaphore_signal(bar, inc=1, device_id=(me, lax.rem(col + k, NCOL)), device_id_type=MESH)

    def remote(src, dst, ssem, rsem, dev):
        pltpu.make_async_remote_copy(
            src_ref=src, dst_ref=dst, send_sem=ssem, recv_sem=rsem, device_id=dev, device_id_type=MESH
        ).start()

    def wait(ref, sem):
        pltpu.make_async_copy(ref, ref, sem).wait()

    lane256 = iota((LEAF, PANEL), 1) // RANK
    row256 = iota((LEAF, PANEL), 0)

    l_kry.wait()
    l_cb.wait()
    l_tr.wait()
    for k in range(4):
        child = 4 * col + k
        prod = lax.dot_general(
            tr[child], cb[child].astype(F32), (((0,), (0,)), ((), ())),
            precision=lax.Precision.HIGHEST, preferred_element_type=F32,
        )
        hi, lo = split(prod)
        pb[0, RANK * k : RANK * (k + 1), :] = hi
        pb[1, RANK * k : RANK * (k + 1), :] = lo
    for c in l_bf:
        c.wait()

    far_pick = (row256 == 4 * lane256 + col).astype(F32)
    par_pick = (row256 == 4 * col + lane256).astype(F32)

    def coefficients(vb):
        a = nt(vb, bfar[...].reshape(4 * RANK, PANEL))
        b = nt(vb, pb[0]) + nt(vb, pb[1])
        a = jnp.sum(a * far_pick, axis=0, keepdims=True)
        b = jnp.sum(b * par_pick, axis=0, keepdims=True)
        return a[:, :128], a[:, 128:], fold(b)

    def set_pay(step, v, extra):
        vb = v.astype(BF16)
        c0, c1, p = coefficients(vb)
        pay[step, 0:1, :] = c0
        pay[step, 1:2, :] = c1
        low = iota((1, 128), 1) < RANK
        pay[step, 2:3, :] = jnp.where(low, p, extra) if extra is not None else p
        halo_src[step] = vb
        vpad[step, LEAF : 2 * LEAF, :] = vb.astype(F32)

    for k in range(KRY):
        for l in range(k, KRY):
            r = partial_sum(kry[k] * kry[l])
            gram_rows[8 * k + l : 8 * k + l + 1, :] = r
            if l > k:
                gram_rows[8 * l + k : 8 * l + k + 1, :] = r
    set_pay(0, kry[KRY - 1], lanes_of(gram_rows[...], 64))

    pl.semaphore_wait(bar, NROW - 1 + NCOL - 1)

    def send_pay(step):
        tab[step, me] = pay[step]
        to_row(lambda p: remote(pay.at[step], tab.at[step, me], pay_s.at[step], pay_r.at[step], (p, col)))
        up = lax.rem(me + 1, NROW)
        down = lax.rem(me + NROW - 1, NROW)
        remote(halo_src.at[step], halo.at[step, 0], halo_s.at[step, 0], halo_r.at[step, 0], (up, col))
        remote(halo_src.at[step], halo.at[step, 1], halo_s.at[step, 1], halo_r.at[step, 1], (down, col))

    send_pay(0)

    l_fm.wait()
    l_cm.wait()
    for c in l_index:
        c.wait()
    for t in range(5):
        for n in range(4):
            if t < 4:
                four = [fm[16 * t + 4 * n + k] for k in range(4)]
            else:
                four = [cm[4 * n + k] for k in range(4)]
            hi, lo = split(jnp.concatenate(four, axis=1))
            ftile[t, 0, RANK * n : RANK * (n + 1), :] = hi
            ftile[t, 1, RANK * n : RANK * (n + 1), :] = lo
    for j in range(4):
        hi, lo = split(jnp.concatenate([tr[4 * g + j] for g in range(4)], axis=1))
        ttile[0, RANK * j : RANK * (j + 1), :] = hi
        ttile[1, RANK * j : RANK * (j + 1), :] = lo

    for t in range(5):
        for n in range(4):
            row = jnp.zeros((LEAF, PANEL), jnp.int32)
            for k in range(4):
                if t < 4:
                    at = fr_s[16 * t + 4 * n + k] - start
                else:
                    at = cr_s[4 * n + k] - 4 * me
                row = jnp.where(lane256 == k, at, row)
            mine = row256 if t < 4 else row256 // 4
            fmask[t, LEAF * n : LEAF * (n + 1), :] = (row == mine).astype(F32)
    for b in range(FAR):
        half = lax.rem(fc_s[b] // 4, 2)
        fpar[b % 2, b // 2 : b // 2 + 1, :] = jnp.full((1, 128), half, jnp.int32)
    for b in range(COARSE):
        fpar[b % 2, 32 + b // 2 : 33 + b // 2, :] = jnp.zeros((1, 128), jnp.int32)

    diag = (iota((RANK, PANEL), 0) // LEAF == iota((RANK, PANEL), 1) // RANK).astype(F32)

    def near_part(step):
        wait(halo.at[step, 0], halo_r.at[step, 0])
        wait(halo.at[step, 1], halo_r.at[step, 1])
        vpad[step, 0:LEAF, :] = halo[step, 0].astype(F32)
        vpad[step, 2 * LEAF :, :] = halo[step, 1].astype(F32)

        def body(i, acc):
            out = jnp.zeros((LEAF, PANEL), F32)
            for s in range(2):
                at = jnp.minimum(lax.rem(nc_s[s, i] - start + LEAF + LEAVES, LEAVES), 3 * LEAF - 1)
                lhs = jnp.broadcast_to(vpad[step, pl.ds(at, 1), :], (LEAF, PANEL)).astype(BF16)
                out = out + nt(lhs, nb[i, s])
            return jnp.where(row256 == i, out, acc)

        near_src[step] = lax.fori_loop(0, LEAF, body, jnp.zeros((LEAF, PANEL), F32), unroll=4)
        near_tab[step, col] = near_src[step]
        for k in range(1, NCOL):
            remote(near_src.at[step], near_tab.at[step, col], near_s.at[step], near_r.at[step], (me, lax.rem(col + k, NCOL)))

    def product(t, rows, first):
        xs = []
        for n in range(4):
            r = jnp.concatenate([rows[first + 2 * n : first + 2 * n + 1], rows[first + 2 * n + 1 : first + 2 * n + 2]], axis=1)
            xs.append(jnp.broadcast_to(r, (LEAF, PANEL)))
        hi, lo = split(jnp.concatenate(xs, axis=0) * fmask[t])
        o = nt(jnp.concatenate([hi, lo], axis=0), ftile[t, 0])
        return o[:RANK] + o[RANK:] + nt(hi, ftile[t, 1])

    def over_groups(o):
        o = o * diag
        return (o[0:16] + o[16:32]) + (o[32:48] + o[48:64])

    def far_part(step):
        wait(tab.at[step, pl.ds(0, NROW - 1)], pay_r.at[step])
        for b in range(FAR):
            c = fc_s[b]
            grow[b % 2, b // 2 : b // 2 + 1, :] = tab[step, c // LEAF, pl.ds(lax.rem(c, LEAF) // 8, 1), :]
        for b in range(COARSE):
            grow[b % 2, 32 + b // 2 : 33 + b // 2, :] = tab[step, cc_s[b] // 4, 2:3, :]
        low = iota((40, 128), 1) < RANK
        even, odd = grow[0], grow[1]
        rows = jnp.where(
            low,
            jnp.where(fpar[0] == 0, even, pltpu.roll(even, 64, 1)),
            jnp.where(fpar[1] == 1, odd, pltpu.roll(odd, 64, 1)),
        )
        cres = fold(over_groups(product(4, rows, 32)))
        far = product(0, rows, 0) + product(1, rows, 8) + product(2, rows, 16) + product(3, rows, 24)
        hi, lo = split(jnp.concatenate([cres, cres], axis=1) * (lane256 == row256 // 4).astype(F32))
        o = nt(jnp.concatenate([hi, lo], axis=0), ttile[0])
        down = o[:LEAF] + o[LEAF:] + nt(hi, ttile[1])
        total = fold(over_groups(far) + down * (lane256 == lax.rem(row256, 4)).astype(F32))
        far_src[step] = jnp.where(iota((8, 128), 1) < RANK, total[:8], total[8:])
        far_tab[step, col] = far_src[step]
        for k in range(1, NCOL):
            remote(far_src.at[step], far_tab.at[step, col], far_s.at[step], far_r.at[step], (me, lax.rem(col + k, NCOL)))

    def assemble(step, v):
        wait(near_tab.at[step, pl.ds(0, NCOL - 1)], near_r.at[step])
        near = (near_tab[step, 0] + near_tab[step, 1]) + (near_tab[step, 2] + near_tab[step, 3])
        base = sw[...] * v + near
        wait(far_tab.at[step, pl.ds(0, NCOL - 1)], far_r.at[step])
        far = (far_tab[step, 0] + far_tab[step, 1]) + (far_tab[step, 2] + far_tab[step, 3])
        back = pltpu.roll(far, 64, 1)
        low = iota((8, 128), 1) < RANK
        both = jnp.concatenate([jnp.where(low, far, back), jnp.where(low, back, far)], axis=0)
        both = jnp.concatenate([both, both], axis=1).astype(BF16).astype(F32)
        for g in range(4):
            lhs = jnp.where(row256 == 4 * g + lane256, both, 0.0).astype(BF16)
            base = base + jnp.dot(lhs, cb[4 * g : 4 * g + 4].reshape(4 * RANK, PANEL), preferred_element_type=F32)
        return base

    def exchange(step, row):
        sc_src[step] = row
        sc_tab[step, me] = row
        to_row(lambda p: remote(sc_src.at[step], sc_tab.at[step, me], sc_s.at[step], sc_r.at[step], (p, col)))

    def exchanged(step):
        wait(sc_tab.at[step, pl.ds(0, NROW - 1)], sc_r.at[step])
        return jnp.sum(sc_tab[step], axis=0) * (1.0 / COUNT)

    lane1 = iota((1, 128), 1)
    sq = (iota((8, 128), 0) == iota((8, 128), 1))

    def pick(row, k):
        return row[:, k : k + 1]

    l_nb.wait()
    near_part(0)
    far_part(0)
    gsum = jnp.sum(tab[0], axis=0)[2:3] * (1.0 / COUNT)
    gram = jnp.zeros((8, 128), F32)
    for k in range(KRY):
        gram = jnp.where(iota((8, 128), 0) == k, pltpu.roll(gsum, 64 - 8 * k, 1), gram)
    gram = jnp.where(iota((8, 128), 1) < KRY, gram, 0.0)
    l_sw.wait()
    w = assemble(0, kry[KRY - 1])
    sums = [partial_sum(kry[k] * w) for k in range(KRY)] + [partial_sum(w * w)]
    exchange(0, lanes_of(stack_rows(sums, 16), 0))
    tot = exchanged(0)

    def quadratic(tot):
        gh = jnp.sum(gram * tot, axis=1, keepdims=True)
        hcol = jnp.sum(jnp.where(sq, tot, 0.0), axis=1, keepdims=True)
        return jnp.sum(gh * hcol, axis=0, keepdims=True)

    h_row = jnp.where(lane1 < KRY, tot, 0.0)
    hh = jnp.sum(h_row * h_row, axis=1, keepdims=True)
    norm = pick(tot, KRY) - 2.0 * hh + quadratic(h_row)
    beta = jnp.sqrt(jnp.maximum(norm, 0.0) + 1e-06)
    w2 = w
    for k in range(KRY):
        w2 = w2 - pick(tot, k) * kry[k]
    q = w2 / beta
    out_v[0] = q
    line = jnp.where(lane1 == KRY + 1, beta, h_row)
    out_h[0:1, :] = line[:, : KRY + 2]

    set_pay(1, q, None)
    send_pay(1)
    new_gram = [partial_sum(kry[k] * q) for k in range(KRY)] + [partial_sum(q * q)]
    near_part(1)
    far_part(1)
    w = assemble(1, q)
    sums = [partial_sum(kry[k] * w) for k in range(KRY)] + [partial_sum(q * w), partial_sum(w * w)]
    exchange(1, lanes_of(stack_rows(sums + [jnp.zeros((1, 128), F32)] * 6 + new_gram, 32), 0))
    tot = exchanged(1)
    h_all = jnp.where(lane1 <= KRY, tot, 0.0)
    h_row = jnp.where(lane1 < KRY, tot, 0.0)
    g_row = jnp.where(lane1 <= KRY, pltpu.roll(tot, 128 - 16, 1), 0.0)
    hh = jnp.sum(h_all * h_all, axis=1, keepdims=True)
    hg = jnp.sum(h_all * g_row, axis=1, keepdims=True)
    h8 = pick(tot, KRY)
    norm = pick(tot, KRY + 1) - 2.0 * hh + quadratic(h_row) + 2.0 * h8 * hg - h8 * h8 * pick(g_row, KRY)
    beta = jnp.sqrt(jnp.maximum(norm, 0.0) + 1e-06)
    w2 = w - h8 * q
    for k in range(KRY):
        w2 = w2 - pick(tot, k) * kry[k]
    out_v[1] = w2 / beta
    line = jnp.where(lane1 == KRY + 1, beta, h_all)
    out_h[1:2, :] = line[:, : KRY + 2]

    for step in range(2):
        wait(tab.at[step, pl.ds(0, NROW - 1)], pay_s.at[step])
        wait(halo.at[step, 0], halo_s.at[step, 0])
        wait(halo.at[step, 1], halo_s.at[step, 1])
        wait(near_tab.at[step, pl.ds(0, NCOL - 1)], near_s.at[step])
        wait(far_tab.at[step, pl.ds(0, NCOL - 1)], far_s.at[step])
        wait(sc_tab.at[step, pl.ds(0, NROW - 1)], sc_s.at[step])


def shards(krylov, self_weight, cluster_basis, transfer, near_blocks, near_cols, far_row, far_col, far_mat, coarse_row, coarse_col, coarse_mat):
    anywhere = pl.BlockSpec(memory_space=pl.ANY)
    S = pltpu.SMEM
    vmem = pl.BlockSpec(memory_space=pltpu.VMEM)
    V = pltpu.VMEM
    DMA = pltpu.SemaphoreType.DMA
    return pl.pallas_call(
        kernel,
        out_shape=(
            jax.ShapeDtypeStruct((2, LEAF, PANEL), F32),
            jax.ShapeDtypeStruct((2, KRY + 2), F32),
        ),
        in_specs=[anywhere] * 12,
        out_specs=(vmem, vmem),
        scratch_shapes=[
            S((2, LEAF), jnp.int32), S((FAR,), jnp.int32), S((FAR,), jnp.int32), S((COARSE,), jnp.int32), S((COARSE,), jnp.int32),
            V((KRY, LEAF, PANEL), F32),
            V((LEAF, PANEL), F32),
            V((LEAF, RANK, PANEL), BF16),
            V((4, RANK, PANEL), BF16),
            V((LEAF, RANK, RANK), F32),
            V((LEAF, 2, PANEL, PANEL), BF16),
            V((FAR, RANK, RANK), F32),
            V((COARSE, RANK, RANK), F32),
            V((2, 4 * RANK, PANEL), BF16),
            V((5, 2, 4 * RANK, 4 * RANK), BF16),
            V((2, 4 * RANK, 4 * RANK), BF16),
            V((5, 4 * LEAF, 4 * RANK), F32),
            V((2, 40, 128), jnp.int32),
            V((64, 128), F32),
            V((2, 3, 128), F32),
            V((2, NROW, 3, 128), F32),
            V((2, LEAF, PANEL), BF16),
            V((2, 2, LEAF, PANEL), BF16),
            V((2, 3 * LEAF, PANEL), F32),
            V((2, 40, 128), F32),
            V((2, LEAF, PANEL), F32),
            V((2, NCOL, LEAF, PANEL), F32),
            V((2, 8, 128), F32),
            V((2, NCOL, 8, 128), F32),
            V((2, 1, 128), F32),
            V((2, NROW, 1, 128), F32),
            DMA((16,)),
            DMA((2,)), DMA((2,)),
            DMA((2, 2)), DMA((2, 2)),
            DMA((2,)), DMA((2,)),
            DMA((2,)), DMA((2,)),
            DMA((2,)), DMA((2,)),
        ],
        compiler_params=pltpu.CompilerParams(
            collective_id=0, has_side_effects=True, vmem_limit_bytes=60 * 2**20
        ),
        name="hmatrix_gmres",
    )(
        krylov,
        self_weight,
        cluster_basis,
        transfer,
        near_blocks,
        far_mat.reshape(FAR, RANK, RANK),
        coarse_mat.reshape(COARSE, RANK, RANK),
        near_cols.T,
        far_row.reshape(FAR),
        far_col.reshape(FAR),
        coarse_row.reshape(COARSE),
        coarse_col.reshape(COARSE),
    )


def solution(mesh):
    in_specs = (
        P(None, "row", None),
        P("row", None),
        P("row", None, None),
        P("row", None, None),
        P("row", "col", None, None),
        P("row", "col"),
        P("row", "col", None),
        P("row", "col", None),
        P("row", "col", None, None, None),
        P("row", "col", None),
        P("row", "col", None),
        P("row", "col", None, None, None),
    )
    out_specs = (P(None, "row", None), P())
    return jax.shard_map(shards, mesh=mesh, in_specs=in_specs, out_specs=out_specs, check_vma=False)
```

```python
import functools

import jax
import jax.numpy as jnp
from jax import lax
from jax.experimental import pallas as pl
from jax.experimental.pallas import tpu as pltpu
from jax.sharding import PartitionSpec as P

MESH = pl.DeviceIdType.MESH
F32 = jnp.float32
BF16 = jnp.bfloat16

NX, NZ, NCORE, NCOL = 4, 8, 2, 4
NROW = NX * NZ * NCORE
LEAF, PANEL, RANK, KRY = 16, 256, 64, 8
LEAVES = NROW * LEAF
FAR, COARSE = 64, 16
QROWS = 20
COUNT = float(LEAVES * PANEL)


def iota(shape, dim):
    return lax.broadcasted_iota(jnp.int32, shape, dim)


def nt(a, b):
    return lax.dot_general(a, b, (((1,), (1,)), ((), ())), preferred_element_type=F32)


def split(x):
    hi = x.astype(BF16)
    return hi, (x - hi.astype(F32)).astype(BF16)


def fold(x):
    s = x[:, :128] + x[:, 128:]
    return s + pltpu.roll(s, 64, 1)


def partial_sum(x):
    s = x[:8] + x[8:]
    return jnp.sum(s[:, :128] + s[:, 128:], axis=0, keepdims=True)


def lanes_of(rows, first):
    sums = jnp.sum(rows, axis=1, keepdims=True)
    n = rows.shape[0]
    return jnp.sum(jnp.where(iota((n, 128), 1) == iota((n, 128), 0) + first, sums, 0.0), axis=0, keepdims=True)


def stack_rows(rows, n):
    out = jnp.zeros((n, 128), F32)
    at = iota((n, 128), 0)
    for j, r in enumerate(rows):
        out = jnp.where(at == j, r, out)
    return out


def kernel(
    kry_h, sw_h, cb_h, tr_h, nb_h, fm_h, cm_h, nc_h, fr_h, fc_h, cr_h, cc_h,
    out_v, out_h,
    nc_s, fr_s, fc_s, cr_s, cc_s,
    kry, sw, cb, bfar, tr, nb, fm, cm,
    pb, ftile, ttile, fmask, fpar, gram_rows,
    pay, tab_a, tab_b, halo_src, halo, vq, vpad_a, vpad_b, nq, qpay, qtab, qgrow, qrows, grow, near_src, near_tab, far_src, far_tab, sc_src, sc_tab,
    load_sem, pay_s, pay_r, halo_s, halo_r, near_s, near_r, far_s, far_r, sc_s, sc_r, q_s, q_r, qf_s, qf_r, vq_s, vq_r,
):
    tab, vpad = (tab_a, tab_b), (vpad_a, vpad_b)
    me = lax.axis_index("row")
    col = lax.axis_index("col")
    x = me // (NZ * NCORE)
    z = lax.rem(me // NCORE, NZ)
    core = lax.rem(me, NCORE)
    start = me * LEAF

    loads = []

    def load(src, dst):
        c = pltpu.make_async_copy(src, dst, load_sem.at[len(loads)])
        c.start()
        loads.append(c)
        return c

    l_kry = load(kry_h, kry)
    l_cb = load(cb_h, cb)
    l_bf = [load(cb_h.at[4 * k + col], bfar.at[k]) for k in range(4)]
    l_tr = load(tr_h, tr)
    l_fm = load(fm_h, fm)
    l_cm = load(cm_h, cm)
    l_nb = load(nb_h, nb)
    l_sw = load(sw_h, sw)
    l_index = [load(h, s) for h, s in ((nc_h, nc_s), (fr_h, fr_s), (fc_h, fc_s), (cr_h, cr_s), (cc_h, cc_s))]

    bar = pltpu.get_barrier_semaphore()

    def far_peer(k):
        jz = k // (NX * NCORE)
        rest = lax.rem(k, NX * NCORE)
        jx = rest // NCORE
        jc = lax.rem(rest, NCORE)
        dz = NZ // 2 + (1 - 2 * lax.rem(jz, 2)) * ((jz + 1) // 2) + NZ
        dx = NX // 2 + (1 - 2 * lax.rem(jx, 2)) * ((jx + 1) // 2) + NX
        pz = lax.rem(z + dz, NZ)
        px = lax.rem(x + dx, NX)
        pc = lax.rem(core + 1 + jc, NCORE)
        return (px * NZ + pz) * NCORE + pc

    def to_row(body):
        def step(k, c):
            body(far_peer(k))
            return c
        lax.fori_loop(0, NROW - 1, step, 0, unroll=7)

    to_row(lambda p: pl.semaphore_signal(bar, inc=1, device_id=(p, col), device_id_type=MESH))
    for k in range(1, NCOL):
        pl.semaphore_signal(bar, inc=1, device_id=(me, lax.rem(col + k, NCOL)), device_id_type=MESH)

    def remote(src, dst, ssem, rsem, dev):
        pltpu.make_async_remote_copy(
            src_ref=src, dst_ref=dst, send_sem=ssem, recv_sem=rsem, device_id=dev, device_id_type=MESH
        ).start()

    def wait(ref, sem):
        pltpu.make_async_copy(ref, ref, sem).wait()

    lane256 = iota((LEAF, PANEL), 1) // RANK
    row256 = iota((LEAF, PANEL), 0)

    l_kry.wait()
    l_cb.wait()
    l_tr.wait()
    for k in range(4):
        child = 4 * col + k
        prod = lax.dot_general(
            tr[child], cb[child].astype(F32), (((0,), (0,)), ((), ())),
            precision=lax.Precision.HIGHEST, preferred_element_type=F32,
        )
        hi, lo = split(prod)
        pb[0, RANK * k : RANK * (k + 1), :] = hi
        pb[1, RANK * k : RANK * (k + 1), :] = lo
    for c in l_bf:
        c.wait()

    far_pick = (row256 == 4 * lane256 + col).astype(F32)
    par_pick = (row256 == 4 * col + lane256).astype(F32)

    def coefficients(hi, lo):
        n = hi.shape[0] // LEAF
        far = bfar[...].reshape(4 * RANK, PANEL)
        a, b = nt(hi, far), nt(hi, pb[0]) + nt(hi, pb[1])
        if lo is not None:
            a, b = a + nt(lo, far), b + nt(lo, pb[0])
        a = jnp.sum(a.reshape(n, LEAF, PANEL) * far_pick[None], axis=1)
        b = jnp.sum(b.reshape(n, LEAF, PANEL) * par_pick[None], axis=1)
        return a, fold(b)

    low1 = iota((1, 128), 1) < RANK

    def set_pay(step, hi, lo, extra):
        a, p = coefficients(hi, lo)
        pay[step, 0:1, :] = a[:, :128]
        pay[step, 1:2, :] = a[:, 128:]
        pay[step, 2:3, :] = jnp.where(low1, p, extra)

    for k in range(KRY):
        for l in range(k, KRY):
            r = partial_sum(kry[k] * kry[l])
            gram_rows[8 * k + l : 8 * k + l + 1, :] = r
            if l > k:
                gram_rows[8 * l + k : 8 * l + k + 1, :] = r
    last_hi, last_lo = split(kry[KRY - 1])
    set_pay(0, last_hi, None, lanes_of(gram_rows[...], 64))
    halo_src[...] = last_hi
    vpad[0][LEAF : 2 * LEAF, :] = last_hi.astype(F32)
    for i in range(LEAF):
        hi, lo = split(kry[:, i, :])
        vq[LEAF + i] = jnp.concatenate([hi, lo], axis=0)

    pl.semaphore_wait(bar, NROW - 1 + NCOL - 1)

    up = lax.rem(me + 1, NROW)
    down = lax.rem(me + NROW - 1, NROW)

    def send_pay(step):
        tab[step][me] = pay[step]
        to_row(lambda p: remote(pay.at[step], tab[step].at[me], pay_s.at[step], pay_r.at[step], (p, col)))

    def to_neighbours(src, low, high, ssem, rsem):
        remote(src, low, ssem.at[0], rsem.at[0], (up, col))
        remote(src, high, ssem.at[1], rsem.at[1], (down, col))

    to_neighbours(halo_src, halo.at[0], halo.at[1], halo_s.at[0], halo_r.at[0])
    send_pay(0)

    l_fm.wait()
    l_cm.wait()
    for c in l_index:
        c.wait()
    for t in range(5):
        for n in range(4):
            if t < 4:
                four = [fm[16 * t + 4 * n + k] for k in range(4)]
            else:
                four = [cm[4 * n + k] for k in range(4)]
            hi, lo = split(jnp.concatenate(four, axis=1))
            ftile[t, 0, RANK * n : RANK * (n + 1), :] = hi
            ftile[t, 1, RANK * n : RANK * (n + 1), :] = lo
    for j in range(4):
        hi, lo = split(jnp.concatenate([tr[4 * g + j] for g in range(4)], axis=1))
        ttile[0, RANK * j : RANK * (j + 1), :] = hi
        ttile[1, RANK * j : RANK * (j + 1), :] = lo

    for t in range(5):
        for n in range(4):
            row = jnp.zeros((LEAF, PANEL), jnp.int32)
            for k in range(4):
                if t < 4:
                    at = fr_s[16 * t + 4 * n + k] - start
                else:
                    at = cr_s[4 * n + k] - 4 * me
                row = jnp.where(lane256 == k, at, row)
            mine = row256 if t < 4 else row256 // 4
            fmask[t, LEAF * n : LEAF * (n + 1), :] = (row == mine).astype(F32)
    for b in range(FAR):
        half = lax.rem(fc_s[b] // 4, 2)
        fpar[b % 2, b // 2 : b // 2 + 1, :] = jnp.full((1, 128), half, jnp.int32)
    for b in range(COARSE):
        fpar[b % 2, 32 + b // 2 : 33 + b // 2, :] = jnp.zeros((1, 128), jnp.int32)

    chip = me // NCORE
    hi, lo = split(kry[...].reshape(KRY * LEAF, PANEL))
    a, p = coefficients(hi, lo)
    qpay[0:KRY, :] = a[:, :128]
    qpay[KRY : 2 * KRY, :] = a[:, 128:]
    qpay[2 * KRY :, :] = jnp.where(iota((4, 128), 1) < RANK, p[:4], p[4:])
    qtab[core, chip, 0:QROWS, :] = qpay[...]

    def to_chip(k, c):
        peer = far_peer(NCORE * k) // NCORE * NCORE + core
        remote(qpay, qtab.at[core, chip, pl.ds(0, QROWS)], q_s, q_r, (peer, col))
        return c

    lax.fori_loop(0, NROW // NCORE - 1, to_chip, 0, unroll=4)
    own = vq.at[pl.ds(LEAF, LEAF)]
    to_neighbours(own, vq.at[pl.ds(0, LEAF)], vq.at[pl.ds(2 * LEAF, LEAF)], vq_s, vq_r)

    diag = (iota((RANK, PANEL), 0) // LEAF == iota((RANK, PANEL), 1) // RANK).astype(F32)

    def near_at(s, i):
        return jnp.minimum(lax.rem(nc_s[s, i] - start + LEAF + LEAVES, LEAVES), 3 * LEAF - 1)

    def send_near(step, near):
        near_src[step] = near
        near_tab[step, col] = near
        for k in range(1, NCOL):
            remote(near_src.at[step], near_tab.at[step, col], near_s.at[step], near_r.at[step], (me, lax.rem(col + k, NCOL)))

    def near_last():
        def body(i, acc):
            out = jnp.zeros((LEAF, PANEL), F32)
            for s in range(2):
                v = jnp.broadcast_to(vpad[0][pl.ds(near_at(s, i), 1), :], (LEAF, PANEL))
                out = out + nt(v.astype(BF16), nb[i, s])
            return jnp.where(row256 == i, out, acc)

        return lax.fori_loop(0, LEAF, body, jnp.zeros((LEAF, PANEL), F32), unroll=16)

    def near_new():
        def body(i, acc):
            out = jnp.zeros((2 * LEAF, PANEL), F32)
            for s in range(2):
                at = near_at(s, i)
                v = jnp.broadcast_to(vpad[1][pl.ds(at, 1), :], (LEAF, PANEL))
                lhs = jnp.where(row256 < 8, v, v - v.astype(BF16).astype(F32)).astype(BF16)
                out = out + nt(jnp.concatenate([vq[at], lhs], axis=0), nb[i, s])
            nq[:, pl.ds(i, 1), :] = (out[0:8] + out[8:16]).reshape(KRY, 1, PANEL)
            return jnp.where(row256 == i, out[16:17] + out[24:25], acc)

        return lax.fori_loop(0, LEAF, body, jnp.zeros((LEAF, PANEL), F32), unroll=16)

    def product(t, rows, first):
        xs = []
        for n in range(4):
            r = jnp.concatenate([rows[first + 2 * n : first + 2 * n + 1], rows[first + 2 * n + 1 : first + 2 * n + 2]], axis=1)
            xs.append(jnp.broadcast_to(r, (LEAF, PANEL)))
        hi, lo = split(jnp.concatenate(xs, axis=0) * fmask[t])
        o = nt(jnp.concatenate([hi, lo], axis=0), ftile[t, 0])
        return o[:RANK] + o[RANK:] + nt(hi, ftile[t, 1])

    def over_groups(o):
        o = o * diag
        return (o[0:16] + o[16:32]) + (o[32:48] + o[48:64])

    def halves(even, odd):
        return jnp.where(
            iota((40, 128), 1) < RANK,
            jnp.where(fpar[0] == 0, even, pltpu.roll(even, 64, 1)),
            jnp.where(fpar[1] == 1, odd, pltpu.roll(odd, 64, 1)),
        )

    def gather(step):
        for b in range(FAR):
            c = fc_s[b]
            grow[b % 2, b // 2 : b // 2 + 1, :] = tab[step][c // LEAF, pl.ds(lax.rem(c, LEAF) // 8, 1), :]
        for b in range(COARSE):
            grow[b % 2, 32 + b // 2 : 33 + b // 2, :] = tab[step][cc_s[b] // 4, 2:3, :]
        return grow[0], grow[1]

    def gather_given():
        for b in range(FAR):
            c = fc_s[b]
            r = c // LEAF
            second = jnp.full((KRY, 128), lax.rem(c, LEAF), jnp.int32) >= LEAF // 2
            both = qtab[lax.rem(r, NCORE), r // NCORE, 0 : 2 * KRY, :]
            qgrow[b % 2, b // 2] = jnp.where(second, both[KRY:], both[:KRY])
        for b in range(COARSE):
            r = cc_s[b] // 4
            pair = qtab[lax.rem(r, NCORE), r // NCORE, 2 * KRY : QROWS, :]
            turned = pltpu.roll(pair, 64, 1)
            low = iota((4, 128), 1) < RANK
            qgrow[b % 2, 32 + b // 2, 0:4, :] = jnp.where(low, pair, turned)
            qgrow[b % 2, 32 + b // 2, 4:8, :] = jnp.where(low, turned, pair)
        for k in range(KRY):
            for p in range(2):
                qrows[k, p] = qgrow[p, :, k, :]

    def far_part(step, even, odd):
        rows = halves(even, odd)
        cres = fold(over_groups(product(4, rows, 32)))
        far = product(0, rows, 0) + product(1, rows, 8) + product(2, rows, 16) + product(3, rows, 24)
        hi, lo = split(jnp.concatenate([cres, cres], axis=1) * (lane256 == row256 // 4).astype(F32))
        o = nt(jnp.concatenate([hi, lo], axis=0), ttile[0])
        down = o[:LEAF] + o[LEAF:] + nt(hi, ttile[1])
        total = fold(over_groups(far) + down * (lane256 == lax.rem(row256, 4)).astype(F32))
        far_src[step] = jnp.where(iota((8, 128), 1) < RANK, total[:8], total[8:])
        far_tab[step, col] = far_src[step]
        for k in range(1, NCOL):
            remote(far_src.at[step], far_tab.at[step, col], far_s.at[step], far_r.at[step], (me, lax.rem(col + k, NCOL)))

    def assemble(step, v):
        wait(near_tab.at[step, pl.ds(0, NCOL - 1)], near_r.at[step])
        near = (near_tab[step, 0] + near_tab[step, 1]) + (near_tab[step, 2] + near_tab[step, 3])
        base = sw[...] * v + near
        wait(far_tab.at[step, pl.ds(0, NCOL - 1)], far_r.at[step])
        far = (far_tab[step, 0] + far_tab[step, 1]) + (far_tab[step, 2] + far_tab[step, 3])
        back = pltpu.roll(far, 64, 1)
        low = iota((8, 128), 1) < RANK
        both = jnp.concatenate([jnp.where(low, far, back), jnp.where(low, back, far)], axis=0)
        both = jnp.concatenate([both, both], axis=1).astype(BF16).astype(F32)
        for g in range(4):
            lhs = jnp.where(row256 == 4 * g + lane256, both, 0.0).astype(BF16)
            base = base + jnp.dot(lhs, cb[4 * g : 4 * g + 4].reshape(4 * RANK, PANEL), preferred_element_type=F32)
        return base

    def exchange(row):
        sc_src[...] = row
        sc_tab[me] = row
        to_row(lambda p: remote(sc_src, sc_tab.at[me], sc_s, sc_r, (p, col)))

    lane1 = iota((1, 128), 1)
    sq = (iota((8, 128), 0) == iota((8, 128), 1))

    def pick(row, k):
        return row[:, k : k + 1]

    l_nb.wait()
    for j in range(2):
        wait(halo.at[j], halo_r.at[0, j])
        vpad[0][2 * LEAF * j : 2 * LEAF * j + LEAF, :] = halo[j].astype(F32)
    send_near(0, near_last())
    wait(tab[0].at[pl.ds(0, NROW - 1)], pay_r.at[0])
    far_part(0, *gather(0))
    gsum = jnp.sum(tab[0][...], axis=0)[2:3] * (1.0 / COUNT)
    gram = jnp.zeros((8, 128), F32)
    for k in range(KRY):
        gram = jnp.where(iota((8, 128), 0) == k, pltpu.roll(gsum, 64 - 8 * k, 1), gram)
    gram = jnp.where(iota((8, 128), 1) < KRY, gram, 0.0)
    l_sw.wait()
    w = assemble(0, kry[KRY - 1])

    def quadratic(tot):
        gh = jnp.sum(gram * tot, axis=1, keepdims=True)
        hcol = jnp.sum(jnp.where(sq, tot, 0.0), axis=1, keepdims=True)
        return jnp.sum(gh * hcol, axis=0, keepdims=True)

    vpad[1][LEAF : 2 * LEAF, :] = w
    own = vpad[1].at[pl.ds(LEAF, LEAF)]
    to_neighbours(own, vpad[1].at[pl.ds(0, LEAF)], vpad[1].at[pl.ds(2 * LEAF, LEAF)], halo_s.at[1], halo_r.at[1])
    sums = [partial_sum(kry[k] * w) for k in range(KRY)] + [partial_sum(w * w)]
    hi, lo = split(w)
    set_pay(1, hi, lo, lanes_of(stack_rows(sums, 16), 64))
    send_pay(1)

    some = qtab.at[core, pl.ds(0, NROW // NCORE - 1), pl.ds(0, QROWS)]
    half = qtab.at[core, :, pl.ds(0, QROWS)]
    wait(some, q_r)
    remote(half, half, qf_s, qf_r, (me + 1 - 2 * core, col))
    for j in range(2):
        wait(vpad[1].at[pl.ds(2 * LEAF * j, LEAF)], halo_r.at[1, j])
        wait(vq.at[pl.ds(2 * LEAF * j, LEAF)], vq_r.at[j])
    near = near_new()
    wait(half, qf_r)
    gather_given()

    wait(tab[1].at[pl.ds(0, NROW - 1)], pay_r.at[1])
    tot = pltpu.roll(jnp.sum(tab[1][...], axis=0)[2:3], 64, 1) * (1.0 / COUNT)
    h_row = jnp.where(lane1 < KRY, tot, 0.0)
    hh = jnp.sum(h_row * h_row, axis=1, keepdims=True)
    norm = pick(tot, KRY) - 2.0 * hh + quadratic(h_row)
    beta = jnp.sqrt(jnp.maximum(norm, 0.0) + 1e-06)
    inv = 1.0 / beta
    hs = [pick(tot, k) for k in range(KRY)]

    def less(v, of):
        for k in range(KRY):
            v = v - hs[k] * of[k]
        return v

    send_near(1, less(near, nq) * inv)
    far_part(1, *[less(g, qrows.at[:, p]) * inv for p, g in enumerate(gather(1))])
    q = less(w, kry) / beta
    out_v[0] = q
    line = jnp.where(lane1 == KRY + 1, beta, h_row)
    out_h[0:1, :] = line[:, : KRY + 2]
    new_gram = [partial_sum(kry[k] * q) for k in range(KRY)] + [partial_sum(q * q)]
    w = assemble(1, q)
    sums = [partial_sum(kry[k] * w) for k in range(KRY)] + [partial_sum(q * w), partial_sum(w * w)]
    exchange(lanes_of(stack_rows(sums + [jnp.zeros((1, 128), F32)] * 6 + new_gram, 32), 0))
    wait(sc_tab.at[pl.ds(0, NROW - 1)], sc_r)
    tot = jnp.sum(sc_tab[...], axis=0) * (1.0 / COUNT)
    h_all = jnp.where(lane1 <= KRY, tot, 0.0)
    h_row = jnp.where(lane1 < KRY, tot, 0.0)
    g_row = jnp.where(lane1 <= KRY, pltpu.roll(tot, 128 - 16, 1), 0.0)
    hh = jnp.sum(h_all * h_all, axis=1, keepdims=True)
    hg = jnp.sum(h_all * g_row, axis=1, keepdims=True)
    h8 = pick(tot, KRY)
    norm = pick(tot, KRY + 1) - 2.0 * hh + quadratic(h_row) + 2.0 * h8 * hg - h8 * h8 * pick(g_row, KRY)
    beta = jnp.sqrt(jnp.maximum(norm, 0.0) + 1e-06)
    w2 = w - h8 * q
    for k in range(KRY):
        w2 = w2 - pick(tot, k) * kry[k]
    out_v[1] = w2 / beta
    line = jnp.where(lane1 == KRY + 1, beta, h_all)
    out_h[1:2, :] = line[:, : KRY + 2]

    for step in range(2):
        wait(tab[step].at[pl.ds(0, NROW - 1)], pay_s.at[step])
        wait(near_tab.at[step, pl.ds(0, NCOL - 1)], near_s.at[step])
        wait(far_tab.at[step, pl.ds(0, NCOL - 1)], far_s.at[step])
    for j in range(2):
        wait(halo.at[j], halo_s.at[0, j])
        wait(vpad[1].at[pl.ds(LEAF, LEAF)], halo_s.at[1, j])
        wait(vq.at[pl.ds(LEAF, LEAF)], vq_s.at[j])
    wait(sc_tab.at[pl.ds(0, NROW - 1)], sc_s)
    wait(some, q_s)
    wait(half, qf_s)


def copy_out(v_in, h_in, v_out, h_out):
    v_out[...] = v_in[...]
    h_out[...] = h_in[...]


def shards(krylov, self_weight, cluster_basis, transfer, near_blocks, near_cols, far_row, far_col, far_mat, coarse_row, coarse_col, coarse_mat):
    anywhere = pl.BlockSpec(memory_space=pl.ANY)
    S = pltpu.SMEM
    vmem = pl.BlockSpec(memory_space=pltpu.VMEM)
    V = pltpu.VMEM
    DMA = pltpu.SemaphoreType.DMA
    shapes = (jax.ShapeDtypeStruct((2, LEAF, PANEL), F32), jax.ShapeDtypeStruct((2, KRY + 2), F32))
    vectors, hessen = pl.pallas_call(
        kernel,
        out_shape=shapes,
        in_specs=[anywhere] * 12,
        out_specs=(vmem, vmem),
        scratch_shapes=[
            S((2, LEAF), jnp.int32), S((FAR,), jnp.int32), S((FAR,), jnp.int32), S((COARSE,), jnp.int32), S((COARSE,), jnp.int32),
            V((KRY, LEAF, PANEL), F32),
            V((LEAF, PANEL), F32),
            V((LEAF, RANK, PANEL), BF16),
            V((4, RANK, PANEL), BF16),
            V((LEAF, RANK, RANK), F32),
            V((LEAF, 2, PANEL, PANEL), BF16),
            V((FAR, RANK, RANK), F32),
            V((COARSE, RANK, RANK), F32),
            V((2, 4 * RANK, PANEL), BF16),
            V((5, 2, 4 * RANK, 4 * RANK), BF16),
            V((2, 4 * RANK, 4 * RANK), BF16),
            V((5, 4 * LEAF, 4 * RANK), F32),
            V((2, 40, 128), jnp.int32),
            V((64, 128), F32),
            V((2, 3, 128), F32),
            V((NROW, 3, 128), F32),
            V((NROW, 3, 128), F32),
            V((LEAF, PANEL), BF16),
            V((2, LEAF, PANEL), BF16),
            V((3 * LEAF, 2 * KRY, PANEL), BF16),
            V((3 * LEAF, PANEL), F32),
            V((3 * LEAF, PANEL), F32),
            V((KRY, LEAF, PANEL), F32),
            V((QROWS, 128), F32),
            V((NCORE, NROW // NCORE, 24, 128), F32),
            V((2, 40, KRY, 128), F32),
            V((KRY, 2, 40, 128), F32),
            V((2, 40, 128), F32),
            V((2, LEAF, PANEL), F32),
            V((2, NCOL, LEAF, PANEL), F32),
            V((2, 8, 128), F32),
            V((2, NCOL, 8, 128), F32),
            V((1, 128), F32),
            V((NROW, 1, 128), F32),
            DMA((16,)),
            DMA((2,)), DMA((2,)),
            DMA((2, 2)), DMA((2, 2)),
            DMA((2,)), DMA((2,)),
            DMA((2,)), DMA((2,)),
            DMA(()), DMA(()),
            DMA(()), DMA(()), DMA(()), DMA(()), DMA((2,)), DMA((2,)),
        ],
        compiler_params=pltpu.CompilerParams(
            collective_id=0, has_side_effects=True, vmem_limit_bytes=60 * 2**20
        ),
        name="hmatrix_gmres",
    )(
        krylov,
        self_weight,
        cluster_basis,
        transfer,
        near_blocks,
        far_mat.reshape(FAR, RANK, RANK),
        coarse_mat.reshape(COARSE, RANK, RANK),
        near_cols.T,
        far_row.reshape(FAR),
        far_col.reshape(FAR),
        coarse_row.reshape(COARSE),
        coarse_col.reshape(COARSE),
    )
    return pl.pallas_call(
        copy_out,
        out_shape=shapes,
        in_specs=[vmem] * 2,
        out_specs=(vmem, vmem),
        compiler_params=pltpu.CompilerParams(vmem_limit_bytes=60 * 2**20),
        name="results",
    )(vectors, hessen)


def solution(mesh):
    in_specs = (
        P(None, "row", None),
        P("row", None),
        P("row", None, None),
        P("row", None, None),
        P("row", "col", None, None),
        P("row", "col"),
        P("row", "col", None),
        P("row", "col", None),
        P("row", "col", None, None, None),
        P("row", "col", None),
        P("row", "col", None),
        P("row", "col", None, None, None),
    )
    out_specs = (P(None, "row", None), P())
    return jax.shard_map(shards, mesh=mesh, in_specs=in_specs, out_specs=out_specs, check_vma=False)
```

```python
import functools

import jax
import jax.numpy as jnp
from jax import lax
from jax.experimental import pallas as pl
from jax.experimental.pallas import tpu as pltpu
from jax.sharding import PartitionSpec as P

MESH = pl.DeviceIdType.MESH
F32 = jnp.float32
BF16 = jnp.bfloat16

NX, NZ, NCORE, NCOL = 4, 8, 2, 4
NROW = NX * NZ * NCORE
LEAF, PANEL, RANK, KRY = 16, 256, 64, 8
LEAVES = NROW * LEAF
FAR, COARSE = 64, 16
QROWS = 21
COUNT = float(LEAVES * PANEL)


def iota(shape, dim):
    return lax.broadcasted_iota(jnp.int32, shape, dim)


def nt(a, b):
    return lax.dot_general(a, b, (((1,), (1,)), ((), ())), preferred_element_type=F32)


def split(x):
    hi = x.astype(BF16)
    return hi, (x - hi.astype(F32)).astype(BF16)


def fold(x):
    s = x[:, :128] + x[:, 128:]
    return s + pltpu.roll(s, 64, 1)


def partial_sum(x):
    s = x[:8] + x[8:]
    return jnp.sum(s[:, :128] + s[:, 128:], axis=0, keepdims=True)


def lanes_of(rows, first):
    sums = jnp.sum(rows, axis=1, keepdims=True)
    n = rows.shape[0]
    return jnp.sum(jnp.where(iota((n, 128), 1) == iota((n, 128), 0) + first, sums, 0.0), axis=0, keepdims=True)


def totals(pairs):
    eights = []
    for x, _ in pairs:
        s = x[:8] + x[8:]
        eights.append(s[:, :128] + s[:, 128:])
    sums = jnp.sum(jnp.concatenate(eights, axis=0), axis=1, keepdims=True)
    lane = iota((8, 128), 1)
    out = jnp.zeros((8, 128), F32)
    for j, (_, at) in enumerate(pairs):
        out = jnp.where(lane == at, sums[8 * j : 8 * j + 8], out)
    return jnp.sum(out, axis=0, keepdims=True)


def tree(x):
    n = x.shape[0]
    while n > 1:
        n //= 2
        x = x[:n] + x[n:]
    return x[0]


def kernel(
    kry_h, sw_h, cb_h, tr_h, nb_h, fm_h, cm_h, nc_h, fr_h, fc_h, cr_h, cc_h,
    out_v, out_h,
    nc_s, fr_s, fc_s, cr_s, cc_s, row_s, half_s,
    kry, sw, cb, bfar, tr, nb, fm, cm,
    pb, ftile, ttile, fmask, adds_to, fpar, gram_rows,
    pay, tab_a, tab_b, halo_src, halo, vq, vpad_a, vpad_b, nq, qpay, qtab, qgrow, qrows, grow, near_src_a, near_src_b, near_tab_a, near_tab_b, far_src, far_tab, sc_src, sc_tab,
    load_sem, pay_s, pay_r, halo_s, halo_r, near_s, near_r, far_s, far_r, sc_s, sc_r, q_s, q_r, qf_s, qf_r, vq_s, vq_r,
):
    tab, vpad = (tab_a, tab_b), (vpad_a, vpad_b)
    me = lax.axis_index("row")
    col = lax.axis_index("col")
    x = me // (NZ * NCORE)
    z = lax.rem(me // NCORE, NZ)
    core = lax.rem(me, NCORE)
    start = me * LEAF

    bar = pltpu.get_barrier_semaphore()

    def far_peer(k):
        jz = k // (NX * NCORE)
        rest = lax.rem(k, NX * NCORE)
        jx = rest // NCORE
        jc = lax.rem(rest, NCORE)
        dz = NZ // 2 + (1 - 2 * lax.rem(jz, 2)) * ((jz + 1) // 2) + NZ
        dx = NX // 2 + (1 - 2 * lax.rem(jx, 2)) * ((jx + 1) // 2) + NX
        pz = lax.rem(z + dz, NZ)
        px = lax.rem(x + dx, NX)
        pc = lax.rem(core + 1 + jc, NCORE)
        return (px * NZ + pz) * NCORE + pc

    def to_row(body):
        def step(k, c):
            body(far_peer(k))
            return c
        lax.fori_loop(0, NROW - 1, step, 0, unroll=7)

    to_row(lambda p: pl.semaphore_signal(bar, inc=1, device_id=(p, col), device_id_type=MESH))
    for k in range(1, NCOL):
        pl.semaphore_signal(bar, inc=1, device_id=(me, lax.rem(col + k, NCOL)), device_id_type=MESH)

    loads = []

    def load(src, dst):
        c = pltpu.make_async_copy(src, dst, load_sem.at[len(loads)])
        c.start()
        loads.append(c)
        return c

    l_kry = load(kry_h, kry)
    l_cb = load(cb_h, cb)
    l_bf = [load(cb_h.at[4 * k + col], bfar.at[k]) for k in range(4)]
    l_tr = load(tr_h, tr)
    def remote(src, dst, ssem, rsem, dev):
        pltpu.make_async_remote_copy(
            src_ref=src, dst_ref=dst, send_sem=ssem, recv_sem=rsem, device_id=dev, device_id_type=MESH
        ).start()

    def wait(ref, sem):
        pltpu.make_async_copy(ref, ref, sem).wait()

    lane256 = iota((LEAF, PANEL), 1) // RANK
    row256 = iota((LEAF, PANEL), 0)

    l_kry.wait()
    l_cb.wait()
    l_tr.wait()
    for k in range(4):
        child = 4 * col + k
        terms = jnp.concatenate(split(tr[child].T), axis=0)
        prod = jnp.dot(terms, cb[child], preferred_element_type=F32)
        hi, lo = split(prod[:RANK] + prod[RANK:])
        pb[0, RANK * k : RANK * (k + 1), :] = hi
        pb[1, RANK * k : RANK * (k + 1), :] = lo
    for c in l_bf:
        c.wait()
    l_index = [load(h, s) for h, s in ((nc_h, nc_s), (fr_h, fr_s), (fc_h, fc_s), (cr_h, cr_s), (cc_h, cc_s))]
    l_fm = load(fm_h, fm)
    l_cm = load(cm_h, cm)
    l_nb = load(nb_h, nb)
    l_sw = load(sw_h, sw)

    far_pick = (row256 == 4 * lane256 + col).astype(F32)
    par_pick = (row256 == 4 * col + lane256).astype(F32)

    def coefficients(hi, lo):
        n = hi.shape[0] // LEAF
        far = bfar[...].reshape(4 * RANK, PANEL)
        a, b = nt(hi, far), nt(hi, pb[0]) + nt(hi, pb[1])
        if lo is not None:
            a, b = a + nt(lo, far), b + nt(lo, pb[0])
        a = jnp.sum(a.reshape(n, LEAF, PANEL) * far_pick[None], axis=1)
        b = jnp.sum(b.reshape(n, LEAF, PANEL) * par_pick[None], axis=1)
        return a, fold(b)

    low1 = iota((1, 128), 1) < RANK

    def set_pay(step, hi, lo, extra):
        a, p = coefficients(hi, lo)
        pay[step, 0:1, :] = a[:, :128]
        pay[step, 1:2, :] = a[:, 128:]
        pay[step, 2:3, :] = jnp.where(low1, p, extra)

    last_hi = kry[KRY - 1].astype(BF16)
    set_pay(0, last_hi, None, jnp.zeros((1, 128), F32))
    halo_src[...] = last_hi
    vpad[0][LEAF : 2 * LEAF, :] = last_hi.astype(F32)
    for i in range(LEAF):
        hi, lo = split(kry[:, i, :])
        vq[LEAF + i] = jnp.concatenate([hi, lo], axis=0)

    pl.semaphore_wait(bar, NROW - 1 + NCOL - 1)

    up = lax.rem(me + 1, NROW)
    down = lax.rem(me + NROW - 1, NROW)

    def send_pay(step):
        tab[step][me] = pay[step]
        to_row(lambda p: remote(pay.at[step], tab[step].at[me], pay_s.at[step], pay_r.at[step], (p, col)))

    def to_neighbours(src, low, high, ssem, rsem):
        remote(src, low, ssem.at[0], rsem.at[0], (up, col))
        remote(src, high, ssem.at[1], rsem.at[1], (down, col))

    to_neighbours(halo_src, halo.at[0], halo.at[1], halo_s.at[0], halo_r.at[0])
    send_pay(0)

    own = vq.at[pl.ds(LEAF, LEAF)]
    to_neighbours(own, vq.at[pl.ds(0, LEAF)], vq.at[pl.ds(2 * LEAF, LEAF)], vq_s, vq_r)

    for k in range(KRY):
        for l in range(k, KRY):
            r = partial_sum(kry[k] * kry[l])
            gram_rows[8 * k + l : 8 * k + l + 1, :] = r
            if l > k:
                gram_rows[8 * l + k : 8 * l + k + 1, :] = r
    chip = me // NCORE
    hi, lo = split(kry[...].reshape(KRY * LEAF, PANEL))
    a, p = coefficients(hi, lo)
    qpay[0:KRY, :] = a[:, :128]
    qpay[KRY : 2 * KRY, :] = a[:, 128:]
    qpay[QROWS - 1 :, :] = lanes_of(gram_rows[...], 64)
    qpay[2 * KRY : QROWS - 1, :] = jnp.where(iota((4, 128), 1) < RANK, p[:4], p[4:])
    qtab[core, chip, 0:QROWS, :] = qpay[...]

    def to_chip(k, c):
        peer = far_peer(NCORE * k) // NCORE * NCORE + core
        remote(qpay, qtab.at[core, chip, pl.ds(0, QROWS)], q_s, q_r, (peer, col))
        return c

    lax.fori_loop(0, NROW // NCORE - 1, to_chip, 0, unroll=4)
    l_fm.wait()
    l_cm.wait()
    for c in l_index:
        c.wait()
    for t in range(5):
        for n in range(4):
            if t < 4:
                four = [fm[16 * t + 4 * n + k] for k in range(4)]
            else:
                four = [cm[4 * n + k] for k in range(4)]
            hi, lo = split(jnp.concatenate(four, axis=1))
            ftile[t, 0, RANK * n : RANK * (n + 1), :] = hi
            ftile[t, 1, RANK * n : RANK * (n + 1), :] = lo
    for j in range(4):
        hi, lo = split(jnp.concatenate([tr[4 * g + j] for g in range(4)], axis=1))
        ttile[0, RANK * j : RANK * (j + 1), :] = hi
        ttile[1, RANK * j : RANK * (j + 1), :] = lo

    for n in range(4):
        row = jnp.zeros((LEAF, PANEL), jnp.int32)
        for k in range(4):
            row = jnp.where(lane256 == k, cr_s[4 * n + k] - 4 * me, row)
        fmask[LEAF * n : LEAF * (n + 1), :] = (row == row256 // 4).astype(F32)
    at = iota((LEAF, FAR), 1)
    row = jnp.zeros((LEAF, FAR), jnp.int32)
    for t in range(4):
        for odd in range(2):
            for n in range(4):
                for pair in range(2):
                    row = jnp.where(at == 16 * t + 8 * odd + 2 * n + pair, fr_s[16 * t + 4 * n + 2 * pair + odd] - start, row)
    adds = (row == iota((LEAF, FAR), 0)).astype(F32)
    adds_to[...] = jnp.concatenate([adds, adds], axis=1).astype(BF16)
    for b in range(FAR):
        within = lax.rem(fc_s[b], LEAF)
        row_s[b] = fc_s[b] // LEAF
        half_s[b] = within // 8
        half = lax.rem(within // 4, 2)
        fpar[b % 2, b // 2 : b // 2 + 1, :] = jnp.full((1, 128), half, jnp.int32)
    for b in range(COARSE):
        row_s[FAR + b] = cc_s[b] // 4
        fpar[b % 2, 32 + b // 2 : 33 + b // 2, :] = jnp.zeros((1, 128), jnp.int32)

    diag = (iota((RANK, PANEL), 0) // LEAF == iota((RANK, PANEL), 1) // RANK).astype(F32)

    def near_at(s, i):
        return jnp.minimum(lax.rem(nc_s[s, i] - start + LEAF + LEAVES, LEAVES), 3 * LEAF - 1)

    near_src, near_tab = (near_src_a, near_src_b), (near_tab_a, near_tab_b)

    def send_near(step, near):
        src, held = near_src[step], near_tab[step]
        src[...] = near.astype(src.dtype)
        held[col] = src[...]
        for k in range(1, NCOL):
            remote(src, held.at[col], near_s.at[step], near_r.at[step], (me, lax.rem(col + k, NCOL)))

    def near_last():
        def body(i, acc):
            out = jnp.zeros((LEAF, PANEL), F32)
            for s in range(2):
                v = jnp.broadcast_to(vpad[0][pl.ds(near_at(s, i), 1), :], (LEAF, PANEL))
                out = out + nt(v.astype(BF16), nb[i, s])
            return jnp.where(row256 == i, out, acc)

        return lax.fori_loop(0, LEAF, body, jnp.zeros((LEAF, PANEL), F32), unroll=16)

    def near_new():
        def body(i, acc):
            out = jnp.zeros((2 * LEAF, PANEL), F32)
            for s in range(2):
                at = near_at(s, i)
                v = jnp.broadcast_to(vpad[1][pl.ds(at, 1), :], (LEAF, PANEL))
                lhs = jnp.where(row256 < 8, v, v - v.astype(BF16).astype(F32)).astype(BF16)
                out = out + nt(jnp.concatenate([vq[at], lhs], axis=0), nb[i, s])
            nq[:, pl.ds(i, 1), :] = (out[0:8] + out[8:16]).reshape(KRY, 1, PANEL)
            return jnp.where(row256 == i, out[16:17] + out[24:25], acc)

        return lax.fori_loop(0, LEAF, body, jnp.zeros((LEAF, PANEL), F32), unroll=16)

    def product(t, rows, first):
        xs = []
        for n in range(4):
            r = jnp.concatenate([rows[first + 2 * n : first + 2 * n + 1], rows[first + 2 * n + 1 : first + 2 * n + 2]], axis=1)
            xs.append(jnp.broadcast_to(r, (LEAF, PANEL)))
        hi, lo = split(jnp.concatenate(xs, axis=0) * fmask[...])
        o = nt(jnp.concatenate([hi, lo], axis=0), ftile[t, 0])
        return o[:RANK] + o[RANK:] + nt(hi, ftile[t, 1])

    row16, lane128 = iota((LEAF, 128), 0), iota((LEAF, 128), 1)
    own_half = ((row16 // 8) == (lane128 // RANK)).astype(F32)
    own_pair = [own_half * (lax.rem(row16, 2) == j).astype(F32) for j in range(2)]
    own_group = (lax.rem(row256, 8) // 2 == lane256).astype(F32)

    def block_results(t, rows):
        both = jnp.concatenate([rows, rows], axis=0)
        hi, lo = split(jnp.concatenate([both * own_pair[0], both * own_pair[1]], axis=1))
        o = nt(jnp.concatenate([hi, lo], axis=0), ftile[t, 0])
        return fold((o[:LEAF] + o[LEAF:] + nt(hi, ftile[t, 1])) * own_group)

    def over_groups(o):
        o = o * diag
        return (o[0:16] + o[16:32]) + (o[32:48] + o[48:64])

    def halves(even, odd):
        return jnp.where(
            iota((40, 128), 1) < RANK,
            jnp.where(fpar[0] == 0, even, pltpu.roll(even, 64, 1)),
            jnp.where(fpar[1] == 1, odd, pltpu.roll(odd, 64, 1)),
        )

    def gather(step):
        for b in range(FAR):
            grow[b % 2, b // 2 : b // 2 + 1, :] = tab[step][row_s[b], pl.ds(half_s[b], 1), :]
        for b in range(COARSE):
            grow[b % 2, 32 + b // 2 : 33 + b // 2, :] = tab[step][row_s[FAR + b], 2:3, :]
        return grow[0], grow[1]

    def gather_given():
        for b in range(FAR):
            r = row_s[b]
            second = jnp.full((KRY, 128), half_s[b], jnp.int32) == 1
            both = qtab[lax.rem(r, NCORE), r // NCORE, 0 : 2 * KRY, :]
            qgrow[b % 2, b // 2] = jnp.where(second, both[KRY:], both[:KRY])
        for b in range(COARSE):
            r = row_s[FAR + b]
            pair = qtab[lax.rem(r, NCORE), r // NCORE, 2 * KRY : QROWS - 1, :]
            turned = pltpu.roll(pair, 64, 1)
            low = iota((4, 128), 1) < RANK
            qgrow[b % 2, 32 + b // 2, 0:4, :] = jnp.where(low, pair, turned)
            qgrow[b % 2, 32 + b // 2, 4:8, :] = jnp.where(low, turned, pair)
        for k in range(KRY):
            for p in range(2):
                qrows[k, p] = qgrow[p, :, k, :]

    def far_part(step, even, odd):
        rows = halves(even, odd)
        cres = fold(over_groups(product(4, rows, 32)))
        blocks = jnp.concatenate([block_results(t, rows[8 * t : 8 * t + 8]) for t in range(4)], axis=0)
        far = jnp.dot(adds_to[...], jnp.concatenate(split(blocks), axis=0), preferred_element_type=F32)
        hi, lo = split(jnp.concatenate([cres, cres], axis=1) * (lane256 == row256 // 4).astype(F32))
        o = nt(jnp.concatenate([hi, lo], axis=0), ttile[0])
        down = o[:LEAF] + o[LEAF:] + nt(hi, ttile[1])
        total = far + fold(down * (lane256 == lax.rem(row256, 4)).astype(F32))
        far_src[step] = jnp.where(iota((8, 128), 1) < RANK, total[:8], total[8:])
        far_tab[step, col] = far_src[step]
        for k in range(1, NCOL):
            remote(far_src.at[step], far_tab.at[step, col], far_s.at[step], far_r.at[step], (me, lax.rem(col + k, NCOL)))

    back_mask = jnp.concatenate([(row256 == 4 * g + lane256).astype(F32) for g in range(4)], axis=1)

    def assemble(step, v, scale):
        wait(near_tab[step].at[pl.ds(0, NCOL - 1)], near_r.at[step])
        parts = [near_tab[step][c].astype(F32) for c in range(NCOL)]
        near = (parts[0] + parts[1]) + (parts[2] + parts[3])
        if scale is not None:
            near = near * scale
        base = sw[...] * v + near
        wait(far_tab.at[step, pl.ds(0, NCOL - 1)], far_r.at[step])
        far = (far_tab[step, 0] + far_tab[step, 1]) + (far_tab[step, 2] + far_tab[step, 3])
        if scale is not None:
            far = far * scale
        back = pltpu.roll(far, 64, 1)
        low = iota((8, 128), 1) < RANK
        both = jnp.concatenate([jnp.where(low, far, back), jnp.where(low, back, far)], axis=0)
        lhs = (jnp.concatenate([both] * 8, axis=1) * back_mask).astype(BF16)
        return base + jnp.dot(lhs, cb[...].reshape(LEAF * RANK, PANEL), preferred_element_type=F32)

    def exchange(row):
        sc_src[...] = row
        sc_tab[me] = row
        to_row(lambda p: remote(sc_src, sc_tab.at[me], sc_s, sc_r, (p, col)))

    lane1 = iota((1, 128), 1)
    sq = (iota((8, 128), 0) == iota((8, 128), 1))

    def pick(row, k):
        return row[:, k : k + 1]

    l_nb.wait()
    for j in range(2):
        wait(halo.at[j], halo_r.at[0, j])
        vpad[0][2 * LEAF * j : 2 * LEAF * j + LEAF, :] = halo[j].astype(F32)
    send_near(0, near_last())
    wait(tab[0].at[pl.ds(0, NROW - 1)], pay_r.at[0])
    far_part(0, *gather(0))
    l_sw.wait()
    w = assemble(0, kry[KRY - 1], None)

    def quadratic(tot):
        gh = jnp.sum(gram * tot, axis=1, keepdims=True)
        hcol = jnp.sum(jnp.where(sq, tot, 0.0), axis=1, keepdims=True)
        return jnp.sum(gh * hcol, axis=0, keepdims=True)

    vpad[1][LEAF : 2 * LEAF, :] = w
    own = vpad[1].at[pl.ds(LEAF, LEAF)]
    to_neighbours(own, vpad[1].at[pl.ds(0, LEAF)], vpad[1].at[pl.ds(2 * LEAF, LEAF)], halo_s.at[1], halo_r.at[1])
    hi, lo = split(w)
    set_pay(1, hi, lo, totals([(kry[k] * w, RANK + k) for k in range(KRY)] + [(w * w, RANK + KRY)]))
    send_pay(1)

    some = qtab.at[core, pl.ds(0, NROW // NCORE - 1), pl.ds(0, QROWS)]
    half = qtab.at[core, :, pl.ds(0, QROWS)]
    wait(some, q_r)
    remote(half, half, qf_s, qf_r, (me + 1 - 2 * core, col))
    for j in range(2):
        wait(vpad[1].at[pl.ds(2 * LEAF * j, LEAF)], halo_r.at[1, j])
        wait(vq.at[pl.ds(2 * LEAF * j, LEAF)], vq_r.at[j])
    near = near_new()
    wait(half, qf_r)
    gather_given()
    gsum = jnp.sum(qtab[:, :, QROWS - 1 : QROWS, :].reshape(NROW, 1, 128), axis=0) * (1.0 / COUNT)
    gram = jnp.zeros((8, 128), F32)
    for k in range(KRY):
        gram = jnp.where(iota((8, 128), 0) == k, pltpu.roll(gsum, 64 - 8 * k, 1), gram)
    gram = jnp.where(iota((8, 128), 1) < KRY, gram, 0.0)

    wait(tab[1].at[pl.ds(0, NROW - 1)], pay_r.at[1])
    tot = pltpu.roll(tree(tab[1][...])[2:3], 64, 1) * (1.0 / COUNT)
    h_row = jnp.where(lane1 < KRY, tot, 0.0)
    hh = jnp.sum(h_row * h_row, axis=1, keepdims=True)
    norm = pick(tot, KRY) - 2.0 * hh + quadratic(h_row)
    beta = jnp.sqrt(jnp.maximum(norm, 0.0) + 1e-06)
    inv = 1.0 / beta
    hs = [pick(tot, k) for k in range(KRY)]

    def less(v, of):
        for k in range(KRY):
            v = v - hs[k] * of[k]
        return v

    send_near(1, less(near, nq))
    far_part(1, *[less(g, qrows.at[:, p]) for p, g in enumerate(gather(1))])
    q = less(w, kry) * inv
    out_v[0] = q
    line = jnp.where(lane1 == KRY + 1, beta, h_row)
    out_h[0:1, :] = line[:, : KRY + 2]
    new_gram = totals([(kry[k] * q, 16 + k) for k in range(KRY)] + [(q * q, 16 + KRY)])
    w = assemble(1, q, inv)
    exchange(new_gram + totals([(kry[k] * w, k) for k in range(KRY)] + [(q * w, KRY), (w * w, KRY + 1)]))
    wait(sc_tab.at[pl.ds(0, NROW - 1)], sc_r)
    tot = tree(sc_tab[...]) * (1.0 / COUNT)
    h_all = jnp.where(lane1 <= KRY, tot, 0.0)
    h_row = jnp.where(lane1 < KRY, tot, 0.0)
    g_row = jnp.where(lane1 <= KRY, pltpu.roll(tot, 128 - 16, 1), 0.0)
    hh = jnp.sum(h_all * h_all, axis=1, keepdims=True)
    hg = jnp.sum(h_all * g_row, axis=1, keepdims=True)
    h8 = pick(tot, KRY)
    norm = pick(tot, KRY + 1) - 2.0 * hh + quadratic(h_row) + 2.0 * h8 * hg - h8 * h8 * pick(g_row, KRY)
    beta = jnp.sqrt(jnp.maximum(norm, 0.0) + 1e-06)
    w2 = w - h8 * q
    for k in range(KRY):
        w2 = w2 - pick(tot, k) * kry[k]
    out_v[1] = w2 * (1.0 / beta)
    line = jnp.where(lane1 == KRY + 1, beta, h_all)
    out_h[1:2, :] = line[:, : KRY + 2]

    for step in range(2):
        wait(tab[step].at[pl.ds(0, NROW - 1)], pay_s.at[step])
        wait(near_tab[step].at[pl.ds(0, NCOL - 1)], near_s.at[step])
        wait(far_tab.at[step, pl.ds(0, NCOL - 1)], far_s.at[step])
    for j in range(2):
        wait(halo.at[j], halo_s.at[0, j])
        wait(vpad[1].at[pl.ds(LEAF, LEAF)], halo_s.at[1, j])
        wait(vq.at[pl.ds(LEAF, LEAF)], vq_s.at[j])
    wait(sc_tab.at[pl.ds(0, NROW - 1)], sc_s)
    wait(some, q_s)
    wait(half, qf_s)


def copy_out(v_in, h_in, v_out, h_out, sem):
    copies = [pltpu.make_async_copy(v_in, v_out, sem.at[0]), pltpu.make_async_copy(h_in, h_out, sem.at[1])]
    for c in copies:
        c.start()
    for c in copies:
        c.wait()


def shards(krylov, self_weight, cluster_basis, transfer, near_blocks, near_cols, far_row, far_col, far_mat, coarse_row, coarse_col, coarse_mat):
    anywhere = pl.BlockSpec(memory_space=pl.ANY)
    S = pltpu.SMEM
    vmem = pl.BlockSpec(memory_space=pltpu.VMEM)
    V = pltpu.VMEM
    DMA = pltpu.SemaphoreType.DMA
    shapes = (jax.ShapeDtypeStruct((2, LEAF, PANEL), F32), jax.ShapeDtypeStruct((2, KRY + 2), F32))
    vectors, hessen = pl.pallas_call(
        kernel,
        out_shape=(V((2, LEAF, PANEL), F32), V((2, KRY + 2), F32)),
        in_specs=[anywhere] * 12,
        out_specs=(vmem, vmem),
        scratch_shapes=[
            S((2, LEAF), jnp.int32), S((FAR,), jnp.int32), S((FAR,), jnp.int32), S((COARSE,), jnp.int32), S((COARSE,), jnp.int32),
            S((FAR + COARSE,), jnp.int32), S((FAR,), jnp.int32),
            V((KRY, LEAF, PANEL), F32),
            V((LEAF, PANEL), F32),
            V((LEAF, RANK, PANEL), BF16),
            V((4, RANK, PANEL), BF16),
            V((LEAF, RANK, RANK), F32),
            V((LEAF, 2, PANEL, PANEL), BF16),
            V((FAR, RANK, RANK), F32),
            V((COARSE, RANK, RANK), F32),
            V((2, 4 * RANK, PANEL), BF16),
            V((5, 2, 4 * RANK, 4 * RANK), BF16),
            V((2, 4 * RANK, 4 * RANK), BF16),
            V((4 * LEAF, 4 * RANK), F32),
            V((LEAF, 2 * FAR), BF16),
            V((2, 40, 128), jnp.int32),
            V((64, 128), F32),
            V((2, 3, 128), F32),
            V((NROW, 3, 128), F32),
            V((NROW, 3, 128), F32),
            V((LEAF, PANEL), BF16),
            V((2, LEAF, PANEL), BF16),
            V((3 * LEAF, 2 * KRY, PANEL), BF16),
            V((3 * LEAF, PANEL), F32),
            V((3 * LEAF, PANEL), F32),
            V((KRY, LEAF, PANEL), F32),
            V((QROWS, 128), F32),
            V((NCORE, NROW // NCORE, 24, 128), F32),
            V((2, 40, KRY, 128), F32),
            V((KRY, 2, 40, 128), F32),
            V((2, 40, 128), F32),
            V((LEAF, PANEL), F32),
            V((LEAF, PANEL), BF16),
            V((NCOL, LEAF, PANEL), F32),
            V((NCOL, LEAF, PANEL), BF16),
            V((2, 8, 128), F32),
            V((2, NCOL, 8, 128), F32),
            V((1, 128), F32),
            V((NROW, 1, 128), F32),
            DMA((16,)),
            DMA((2,)), DMA((2,)),
            DMA((2, 2)), DMA((2, 2)),
            DMA((2,)), DMA((2,)),
            DMA((2,)), DMA((2,)),
            DMA(()), DMA(()),
            DMA(()), DMA(()), DMA(()), DMA(()), DMA((2,)), DMA((2,)),
        ],
        compiler_params=pltpu.CompilerParams(
            collective_id=0, has_side_effects=True, vmem_limit_bytes=60 * 2**20
        ),
        name="hmatrix_gmres",
    )(
        krylov,
        self_weight,
        cluster_basis,
        transfer,
        near_blocks,
        far_mat.reshape(FAR, RANK, RANK),
        coarse_mat.reshape(COARSE, RANK, RANK),
        near_cols.T,
        far_row.reshape(FAR),
        far_col.reshape(FAR),
        coarse_row.reshape(COARSE),
        coarse_col.reshape(COARSE),
    )
    return pl.pallas_call(
        copy_out,
        out_shape=shapes,
        in_specs=[vmem] * 2,
        out_specs=(anywhere, anywhere),
        scratch_shapes=[DMA((2,))],
        name="results",
    )(pltpu.with_memory_space_constraint(vectors, V), pltpu.with_memory_space_constraint(hessen, V))


def solution(mesh):
    in_specs = (
        P(None, "row", None),
        P("row", None),
        P("row", None, None),
        P("row", None, None),
        P("row", "col", None, None),
        P("row", "col"),
        P("row", "col", None),
        P("row", "col", None),
        P("row", "col", None, None, None),
        P("row", "col", None),
        P("row", "col", None),
        P("row", "col", None, None, None),
    )
    out_specs = (P(None, "row", None), P())
    return jax.shard_map(shards, mesh=mesh, in_specs=in_specs, out_specs=out_specs, check_vma=False)
```

```python
import functools

import jax
import jax.numpy as jnp
from jax import lax
from jax.experimental import pallas as pl
from jax.experimental.pallas import tpu as pltpu
from jax.sharding import PartitionSpec as P

MESH = pl.DeviceIdType.MESH
F32 = jnp.float32
BF16 = jnp.bfloat16

NX, NZ, NCORE, NCOL = 4, 8, 2, 4
NROW = NX * NZ * NCORE
LEAF, PANEL, RANK, KRY = 16, 256, 64, 8
LEAVES = NROW * LEAF
FAR, COARSE = 64, 16
QROWS = 21
COUNT = float(LEAVES * PANEL)


def iota(shape, dim):
    return lax.broadcasted_iota(jnp.int32, shape, dim)


def nt(a, b):
    return lax.dot_general(a, b, (((1,), (1,)), ((), ())), preferred_element_type=F32)


def split(x):
    hi = x.astype(BF16)
    return hi, (x - hi.astype(F32)).astype(BF16)


def fold(x):
    s = x[:, :128] + x[:, 128:]
    return s + pltpu.roll(s, 64, 1)


def partial_sum(x):
    s = x[:8] + x[8:]
    return jnp.sum(s[:, :128] + s[:, 128:], axis=0, keepdims=True)


def lanes_of(rows, first):
    sums = jnp.sum(rows, axis=1, keepdims=True)
    n = rows.shape[0]
    return jnp.sum(jnp.where(iota((n, 128), 1) == iota((n, 128), 0) + first, sums, 0.0), axis=0, keepdims=True)


def totals(pairs):
    eights = []
    for x, _ in pairs:
        s = x[:8] + x[8:]
        eights.append(s[:, :128] + s[:, 128:])
    sums = jnp.sum(jnp.concatenate(eights, axis=0), axis=1, keepdims=True)
    lane = iota((8, 128), 1)
    out = jnp.zeros((8, 128), F32)
    for j, (_, at) in enumerate(pairs):
        out = jnp.where(lane == at, sums[8 * j : 8 * j + 8], out)
    return jnp.sum(out, axis=0, keepdims=True)


def tree(x):
    n = x.shape[0]
    while n > 1:
        n //= 2
        x = x[:n] + x[n:]
    return x[0]


def kernel(
    kry_h, sw_h, cb_h, tr_h, nb_h, fm_h, cm_h, nc_h, fr_h, fc_h, cr_h, cc_h,
    out_v, out_h,
    nc_s, fr_s, fc_s, cr_s, cc_s, row_s, half_s,
    kry, sw, cb, bfar, tr, nb, fm, cm,
    pb, ftile, ttile, fmask, adds_to, fpar, gram_rows,
    pay, tab_a, tab_b, halo_src, halo, vq, vpad_a, vpad_b, nq, qpay, qtab, qgrow, qrows, grow, near_src_a, near_src_b, near_tab_a, near_tab_b, far_src, far_tab, sc_src, sc_tab,
    load_sem, pay_s, pay_r, halo_s, halo_r, near_s, near_r, far_s, far_r, sc_s, sc_r, q_s, q_r, qf_s, qf_r, vq_s, vq_r,
):
    tab, vpad = (tab_a, tab_b), (vpad_a, vpad_b)
    me = lax.axis_index("row")
    col = lax.axis_index("col")
    x = me // (NZ * NCORE)
    z = lax.rem(me // NCORE, NZ)
    core = lax.rem(me, NCORE)
    start = me * LEAF

    bar = pltpu.get_barrier_semaphore()

    def far_peer(k):
        jz = k // (NX * NCORE)
        rest = lax.rem(k, NX * NCORE)
        jx = rest // NCORE
        jc = lax.rem(rest, NCORE)
        dz = NZ // 2 + (1 - 2 * lax.rem(jz, 2)) * ((jz + 1) // 2) + NZ
        dx = NX // 2 + (1 - 2 * lax.rem(jx, 2)) * ((jx + 1) // 2) + NX
        pz = lax.rem(z + dz, NZ)
        px = lax.rem(x + dx, NX)
        pc = lax.rem(core + 1 + jc, NCORE)
        return (px * NZ + pz) * NCORE + pc

    def to_row(body):
        def step(k, c):
            body(far_peer(k))
            return c
        lax.fori_loop(0, NROW - 1, step, 0, unroll=7)

    to_row(lambda p: pl.semaphore_signal(bar, inc=1, device_id=(p, col), device_id_type=MESH))
    for k in range(1, NCOL):
        pl.semaphore_signal(bar, inc=1, device_id=(me, lax.rem(col + k, NCOL)), device_id_type=MESH)

    loads = []

    def load(src, dst):
        c = pltpu.make_async_copy(src, dst, load_sem.at[len(loads)])
        c.start()
        loads.append(c)
        return c

    l_kry = load(kry_h, kry)
    l_cb = load(cb_h, cb)
    l_bf = [load(cb_h.at[4 * k + col], bfar.at[k]) for k in range(4)]
    l_tr = load(tr_h, tr)
    def remote(src, dst, ssem, rsem, dev):
        pltpu.make_async_remote_copy(
            src_ref=src, dst_ref=dst, send_sem=ssem, recv_sem=rsem, device_id=dev, device_id_type=MESH
        ).start()

    def wait(ref, sem):
        pltpu.make_async_copy(ref, ref, sem).wait()

    lane256 = iota((LEAF, PANEL), 1) // RANK
    row256 = iota((LEAF, PANEL), 0)

    l_kry.wait()
    l_cb.wait()
    l_tr.wait()
    for k in range(4):
        child = 4 * col + k
        terms = jnp.concatenate(split(tr[child].T), axis=0)
        prod = jnp.dot(terms, cb[child], preferred_element_type=F32)
        hi, lo = split(prod[:RANK] + prod[RANK:])
        pb[0, RANK * k : RANK * (k + 1), :] = hi
        pb[1, RANK * k : RANK * (k + 1), :] = lo
    for c in l_bf:
        c.wait()
    l_index = [load(h, s) for h, s in ((nc_h, nc_s), (fr_h, fr_s), (fc_h, fc_s), (cr_h, cr_s), (cc_h, cc_s))]
    l_fm = load(fm_h, fm)
    l_cm = load(cm_h, cm)
    l_nb = load(nb_h, nb)
    l_sw = load(sw_h, sw)

    far_pick = (row256 == 4 * lane256 + col).astype(F32)
    par_pick = (row256 == 4 * col + lane256).astype(F32)

    def coefficients(hi, lo):
        n = hi.shape[0] // LEAF
        far = bfar[...].reshape(4 * RANK, PANEL)
        a, b = nt(hi, far), nt(hi, pb[0]) + nt(hi, pb[1])
        if lo is not None:
            a, b = a + nt(lo, far), b + nt(lo, pb[0])
        a = jnp.sum(a.reshape(n, LEAF, PANEL) * far_pick[None], axis=1)
        b = jnp.sum(b.reshape(n, LEAF, PANEL) * par_pick[None], axis=1)
        return a, fold(b)

    low1 = iota((1, 128), 1) < RANK

    def set_pay(step, hi, lo, extra):
        a, p = coefficients(hi, lo)
        pay[step, 0:1, :] = a[:, :128]
        pay[step, 1:2, :] = a[:, 128:]
        pay[step, 2:3, :] = jnp.where(low1, p, extra)

    last_hi = kry[KRY - 1].astype(BF16)
    set_pay(0, last_hi, None, jnp.zeros((1, 128), F32))
    halo_src[...] = last_hi
    vpad[0][LEAF : 2 * LEAF, :] = last_hi.astype(F32)
    for i in range(LEAF):
        hi, lo = split(kry[:, i, :])
        vq[LEAF + i] = jnp.concatenate([hi, lo], axis=0)

    pl.semaphore_wait(bar, NROW - 1 + NCOL - 1)

    up = lax.rem(me + 1, NROW)
    down = lax.rem(me + NROW - 1, NROW)

    def send_pay(step):
        tab[step][me] = pay[step]
        to_row(lambda p: remote(pay.at[step], tab[step].at[me], pay_s.at[step], pay_r.at[step], (p, col)))

    def to_neighbours(src, low, high, ssem, rsem):
        remote(src, low, ssem.at[0], rsem.at[0], (up, col))
        remote(src, high, ssem.at[1], rsem.at[1], (down, col))

    to_neighbours(halo_src, halo.at[0], halo.at[1], halo_s.at[0], halo_r.at[0])
    send_pay(0)

    own = vq.at[pl.ds(LEAF, LEAF)]
    to_neighbours(own, vq.at[pl.ds(0, LEAF)], vq.at[pl.ds(2 * LEAF, LEAF)], vq_s, vq_r)

    for k in range(KRY):
        for l in range(k, KRY):
            r = partial_sum(kry[k] * kry[l])
            gram_rows[8 * k + l : 8 * k + l + 1, :] = r
            if l > k:
                gram_rows[8 * l + k : 8 * l + k + 1, :] = r
    chip = me // NCORE
    hi, lo = split(kry[...].reshape(KRY * LEAF, PANEL))
    a, p = coefficients(hi, lo)
    qpay[0:KRY, :] = a[:, :128]
    qpay[KRY : 2 * KRY, :] = a[:, 128:]
    qpay[QROWS - 1 :, :] = lanes_of(gram_rows[...], 64)
    qpay[2 * KRY : QROWS - 1, :] = jnp.where(iota((4, 128), 1) < RANK, p[:4], p[4:])
    qtab[core, chip, 0:QROWS, :] = qpay[...]

    def to_chip(k, c):
        peer = far_peer(NCORE * k) // NCORE * NCORE + core
        remote(qpay, qtab.at[core, chip, pl.ds(0, QROWS)], q_s, q_r, (peer, col))
        return c

    lax.fori_loop(0, NROW // NCORE - 1, to_chip, 0, unroll=4)
    l_fm.wait()
    l_cm.wait()
    for c in l_index:
        c.wait()
    for t in range(5):
        for n in range(4):
            if t < 4:
                four = [fm[16 * t + 4 * n + k] for k in range(4)]
            else:
                four = [cm[4 * n + k] for k in range(4)]
            hi, lo = split(jnp.concatenate(four, axis=1))
            ftile[t, 0, RANK * n : RANK * (n + 1), :] = hi
            ftile[t, 1, RANK * n : RANK * (n + 1), :] = lo
    for j in range(4):
        hi, lo = split(jnp.concatenate([tr[4 * g + j] for g in range(4)], axis=1))
        ttile[0, RANK * j : RANK * (j + 1), :] = hi
        ttile[1, RANK * j : RANK * (j + 1), :] = lo

    for n in range(4):
        row = jnp.zeros((LEAF, PANEL), jnp.int32)
        for k in range(4):
            row = jnp.where(lane256 == k, cr_s[4 * n + k] - 4 * me, row)
        fmask[LEAF * n : LEAF * (n + 1), :] = (row == row256 // 4).astype(F32)
    at = iota((LEAF, FAR), 1)
    row = jnp.zeros((LEAF, FAR), jnp.int32)
    for t in range(4):
        for odd in range(2):
            for n in range(4):
                for pair in range(2):
                    row = jnp.where(at == 16 * t + 8 * odd + 2 * n + pair, fr_s[16 * t + 4 * n + 2 * pair + odd] - start, row)
    adds = (row == iota((LEAF, FAR), 0)).astype(F32)
    adds_to[...] = jnp.concatenate([adds, adds], axis=1).astype(BF16)
    for b in range(FAR):
        within = lax.rem(fc_s[b], LEAF)
        row_s[b] = fc_s[b] // LEAF
        half_s[b] = within // 8
        half = lax.rem(within // 4, 2)
        fpar[b % 2, b // 2 : b // 2 + 1, :] = jnp.full((1, 128), half, jnp.int32)
    for b in range(COARSE):
        row_s[FAR + b] = cc_s[b] // 4
        fpar[b % 2, 32 + b // 2 : 33 + b // 2, :] = jnp.zeros((1, 128), jnp.int32)

    diag = (iota((RANK, PANEL), 0) // LEAF == iota((RANK, PANEL), 1) // RANK).astype(F32)

    def near_at(s, i):
        return jnp.minimum(lax.rem(nc_s[s, i] - start + LEAF + LEAVES, LEAVES), 3 * LEAF - 1)

    near_src, near_tab = (near_src_a, near_src_b), (near_tab_a, near_tab_b)

    def send_near(step, near):
        src, held = near_src[step], near_tab[step]
        src[...] = near.astype(src.dtype)
        held[col] = src[...]
        for k in range(1, NCOL):
            remote(src, held.at[col], near_s.at[step], near_r.at[step], (me, lax.rem(col + k, NCOL)))

    def near_last():
        def body(i, acc):
            out = jnp.zeros((LEAF, PANEL), F32)
            for s in range(2):
                v = jnp.broadcast_to(vpad[0][pl.ds(near_at(s, i), 1), :], (LEAF, PANEL))
                out = out + nt(v.astype(BF16), nb[i, s])
            return jnp.where(row256 == i, out, acc)

        return lax.fori_loop(0, LEAF, body, jnp.zeros((LEAF, PANEL), F32), unroll=16)

    def near_new():
        def body(i, acc):
            out = jnp.zeros((2 * LEAF, PANEL), F32)
            for s in range(2):
                at = near_at(s, i)
                v = jnp.broadcast_to(vpad[1][pl.ds(at, 1), :], (LEAF, PANEL))
                lhs = jnp.where(row256 < 8, v, v - v.astype(BF16).astype(F32)).astype(BF16)
                out = out + nt(jnp.concatenate([vq[at], lhs], axis=0), nb[i, s])
            nq[:, pl.ds(i, 1), :] = (out[0:8] + out[8:16]).reshape(KRY, 1, PANEL)
            return jnp.where(row256 == i, out[16:17] + out[24:25], acc)

        return lax.fori_loop(0, LEAF, body, jnp.zeros((LEAF, PANEL), F32), unroll=16)

    def product(t, rows, first):
        xs = []
        for n in range(4):
            r = jnp.concatenate([rows[first + 2 * n : first + 2 * n + 1], rows[first + 2 * n + 1 : first + 2 * n + 2]], axis=1)
            xs.append(jnp.broadcast_to(r, (LEAF, PANEL)))
        hi, lo = split(jnp.concatenate(xs, axis=0) * fmask[...])
        o = nt(jnp.concatenate([hi, lo], axis=0), ftile[t, 0])
        return o[:RANK] + o[RANK:] + nt(hi, ftile[t, 1])

    row16, lane128 = iota((LEAF, 128), 0), iota((LEAF, 128), 1)
    own_half = ((row16 // 8) == (lane128 // RANK)).astype(F32)
    own_pair = [own_half * (lax.rem(row16, 2) == j).astype(F32) for j in range(2)]
    own_group = (lax.rem(row256, 8) // 2 == lane256).astype(F32)

    def block_results(t, rows):
        both = jnp.concatenate([rows, rows], axis=0)
        hi, lo = split(jnp.concatenate([both * own_pair[0], both * own_pair[1]], axis=1))
        o = nt(jnp.concatenate([hi, lo], axis=0), ftile[t, 0])
        return fold((o[:LEAF] + o[LEAF:] + nt(hi, ftile[t, 1])) * own_group)

    def over_groups(o):
        o = o * diag
        return (o[0:16] + o[16:32]) + (o[32:48] + o[48:64])

    def halves(even, odd):
        return jnp.where(
            iota((40, 128), 1) < RANK,
            jnp.where(fpar[0] == 0, even, pltpu.roll(even, 64, 1)),
            jnp.where(fpar[1] == 1, odd, pltpu.roll(odd, 64, 1)),
        )

    def gather(step):
        for b in range(FAR):
            grow[b % 2, b // 2 : b // 2 + 1, :] = tab[step][row_s[b], pl.ds(half_s[b], 1), :]
        for b in range(COARSE):
            grow[b % 2, 32 + b // 2 : 33 + b // 2, :] = tab[step][row_s[FAR + b], 2:3, :]
        return grow[0], grow[1]

    def gather_given():
        for b in range(FAR):
            r = row_s[b]
            second = jnp.full((KRY, 128), half_s[b], jnp.int32) == 1
            both = qtab[lax.rem(r, NCORE), r // NCORE, 0 : 2 * KRY, :]
            qgrow[b % 2, b // 2] = jnp.where(second, both[KRY:], both[:KRY])
        for b in range(COARSE):
            r = row_s[FAR + b]
            pair = qtab[lax.rem(r, NCORE), r // NCORE, 2 * KRY : QROWS - 1, :]
            turned = pltpu.roll(pair, 64, 1)
            low = iota((4, 128), 1) < RANK
            qgrow[b % 2, 32 + b // 2, 0:4, :] = jnp.where(low, pair, turned)
            qgrow[b % 2, 32 + b // 2, 4:8, :] = jnp.where(low, turned, pair)
        for k in range(KRY):
            for p in range(2):
                qrows[k, p] = qgrow[p, :, k, :]

    def far_part(step, even, odd):
        rows = halves(even, odd)
        cres = fold(over_groups(product(4, rows, 32)))
        blocks = jnp.concatenate([block_results(t, rows[8 * t : 8 * t + 8]) for t in range(4)], axis=0)
        far = jnp.dot(adds_to[...], jnp.concatenate(split(blocks), axis=0), preferred_element_type=F32)
        hi, lo = split(jnp.concatenate([cres, cres], axis=1) * (lane256 == row256 // 4).astype(F32))
        o = nt(jnp.concatenate([hi, lo], axis=0), ttile[0])
        down = o[:LEAF] + o[LEAF:] + nt(hi, ttile[1])
        total = far + fold(down * (lane256 == lax.rem(row256, 4)).astype(F32))
        far_src[step] = jnp.where(iota((8, 128), 1) < RANK, total[:8], total[8:])
        far_tab[step, col] = far_src[step]
        for k in range(1, NCOL):
            remote(far_src.at[step], far_tab.at[step, col], far_s.at[step], far_r.at[step], (me, lax.rem(col + k, NCOL)))

    back_mask = jnp.concatenate([(row256 == 4 * g + lane256).astype(F32) for g in range(4)], axis=1)

    def assemble(step, v, scale):
        wait(near_tab[step].at[pl.ds(0, NCOL - 1)], near_r.at[step])
        parts = [near_tab[step][c].astype(F32) for c in range(NCOL)]
        near = (parts[0] + parts[1]) + (parts[2] + parts[3])
        if scale is not None:
            near = near * scale
        base = sw[...] * v + near
        wait(far_tab.at[step, pl.ds(0, NCOL - 1)], far_r.at[step])
        far = (far_tab[step, 0] + far_tab[step, 1]) + (far_tab[step, 2] + far_tab[step, 3])
        if scale is not None:
            far = far * scale
        back = pltpu.roll(far, 64, 1)
        low = iota((8, 128), 1) < RANK
        both = jnp.concatenate([jnp.where(low, far, back), jnp.where(low, back, far)], axis=0)
        lhs = (jnp.concatenate([both] * 8, axis=1) * back_mask).astype(BF16)
        return base + jnp.dot(lhs, cb[...].reshape(LEAF * RANK, PANEL), preferred_element_type=F32)

    def exchange(row):
        sc_src[...] = row
        sc_tab[me] = row
        to_row(lambda p: remote(sc_src, sc_tab.at[me], sc_s, sc_r, (p, col)))

    lane1 = iota((1, 128), 1)
    sq = (iota((8, 128), 0) == iota((8, 128), 1))

    def pick(row, k):
        return row[:, k : k + 1]

    l_nb.wait()
    for j in range(2):
        wait(halo.at[j], halo_r.at[0, j])
        vpad[0][2 * LEAF * j : 2 * LEAF * j + LEAF, :] = halo[j].astype(F32)
    send_near(0, near_last())
    wait(tab[0].at[pl.ds(0, NROW - 1)], pay_r.at[0])
    far_part(0, *gather(0))
    l_sw.wait()
    w = assemble(0, kry[KRY - 1], None)

    def quadratic(tot):
        gh = jnp.sum(gram * tot, axis=1, keepdims=True)
        hcol = jnp.sum(jnp.where(sq, tot, 0.0), axis=1, keepdims=True)
        return jnp.sum(gh * hcol, axis=0, keepdims=True)

    vpad[1][LEAF : 2 * LEAF, :] = w
    own = vpad[1].at[pl.ds(LEAF, LEAF)]
    to_neighbours(own, vpad[1].at[pl.ds(0, LEAF)], vpad[1].at[pl.ds(2 * LEAF, LEAF)], halo_s.at[1], halo_r.at[1])
    hi, lo = split(w)
    set_pay(1, hi, lo, totals([(kry[k] * w, RANK + k) for k in range(KRY)] + [(w * w, RANK + KRY)]))
    send_pay(1)

    some = qtab.at[core, pl.ds(0, NROW // NCORE - 1), pl.ds(0, QROWS)]
    half = qtab.at[core, :, pl.ds(0, QROWS)]
    wait(some, q_r)
    remote(half, half, qf_s, qf_r, (me + 1 - 2 * core, col))
    for j in range(2):
        wait(vpad[1].at[pl.ds(2 * LEAF * j, LEAF)], halo_r.at[1, j])
        wait(vq.at[pl.ds(2 * LEAF * j, LEAF)], vq_r.at[j])
    near = near_new()
    wait(half, qf_r)
    gather_given()
    wait(tab[1].at[pl.ds(0, NROW - 1)], pay_r.at[1])
    tot = pltpu.roll(tree(tab[1][...])[2:3], 64, 1) * (1.0 / COUNT)
    hs = [pick(tot, k) for k in range(KRY)]

    def less(v, of):
        for k in range(KRY):
            v = v - hs[k] * of[k]
        return v

    send_near(1, less(near, nq))
    far_part(1, *[less(g, qrows.at[:, p]) for p, g in enumerate(gather(1))])
    gsum = jnp.sum(qtab[:, :, QROWS - 1 : QROWS, :].reshape(NROW, 1, 128), axis=0) * (1.0 / COUNT)
    gram = jnp.zeros((8, 128), F32)
    for k in range(KRY):
        gram = jnp.where(iota((8, 128), 0) == k, pltpu.roll(gsum, 64 - 8 * k, 1), gram)
    gram = jnp.where(iota((8, 128), 1) < KRY, gram, 0.0)
    h_row = jnp.where(lane1 < KRY, tot, 0.0)
    hh = jnp.sum(h_row * h_row, axis=1, keepdims=True)
    norm = pick(tot, KRY) - 2.0 * hh + quadratic(h_row)
    beta = jnp.sqrt(jnp.maximum(norm, 0.0) + 1e-06)
    inv = 1.0 / beta
    q = less(w, kry) * inv
    out_v[0] = q
    line = jnp.where(lane1 == KRY + 1, beta, h_row)
    out_h[0:1, :] = line[:, : KRY + 2]
    new_gram = totals([(kry[k] * q, 16 + k) for k in range(KRY)] + [(q * q, 16 + KRY)])
    w = assemble(1, q, inv)
    exchange(new_gram + totals([(kry[k] * w, k) for k in range(KRY)] + [(q * w, KRY), (w * w, KRY + 1)]))
    wait(sc_tab.at[pl.ds(0, NROW - 1)], sc_r)
    tot = tree(sc_tab[...]) * (1.0 / COUNT)
    h_all = jnp.where(lane1 <= KRY, tot, 0.0)
    h_row = jnp.where(lane1 < KRY, tot, 0.0)
    g_row = jnp.where(lane1 <= KRY, pltpu.roll(tot, 128 - 16, 1), 0.0)
    hh = jnp.sum(h_all * h_all, axis=1, keepdims=True)
    hg = jnp.sum(h_all * g_row, axis=1, keepdims=True)
    h8 = pick(tot, KRY)
    norm = pick(tot, KRY + 1) - 2.0 * hh + quadratic(h_row) + 2.0 * h8 * hg - h8 * h8 * pick(g_row, KRY)
    beta = jnp.sqrt(jnp.maximum(norm, 0.0) + 1e-06)
    w2 = w - h8 * q
    for k in range(KRY):
        w2 = w2 - pick(tot, k) * kry[k]
    out_v[1] = w2 * (1.0 / beta)
    line = jnp.where(lane1 == KRY + 1, beta, h_all)
    out_h[1:2, :] = line[:, : KRY + 2]

    for step in range(2):
        wait(tab[step].at[pl.ds(0, NROW - 1)], pay_s.at[step])
        wait(near_tab[step].at[pl.ds(0, NCOL - 1)], near_s.at[step])
        wait(far_tab.at[step, pl.ds(0, NCOL - 1)], far_s.at[step])
    for j in range(2):
        wait(halo.at[j], halo_s.at[0, j])
        wait(vpad[1].at[pl.ds(LEAF, LEAF)], halo_s.at[1, j])
        wait(vq.at[pl.ds(LEAF, LEAF)], vq_s.at[j])
    wait(sc_tab.at[pl.ds(0, NROW - 1)], sc_s)
    wait(some, q_s)
    wait(half, qf_s)


def copy_out(v_in, h_in, v_out, h_out, sem):
    copies = [pltpu.make_async_copy(v_in, v_out, sem.at[0]), pltpu.make_async_copy(h_in, h_out, sem.at[1])]
    for c in copies:
        c.start()
    for c in copies:
        c.wait()


def shards(krylov, self_weight, cluster_basis, transfer, near_blocks, near_cols, far_row, far_col, far_mat, coarse_row, coarse_col, coarse_mat):
    anywhere = pl.BlockSpec(memory_space=pl.ANY)
    S = pltpu.SMEM
    vmem = pl.BlockSpec(memory_space=pltpu.VMEM)
    V = pltpu.VMEM
    DMA = pltpu.SemaphoreType.DMA
    shapes = (jax.ShapeDtypeStruct((2, LEAF, PANEL), F32), jax.ShapeDtypeStruct((2, KRY + 2), F32))
    vectors, hessen = pl.pallas_call(
        kernel,
        out_shape=(V((2, LEAF, PANEL), F32), V((2, KRY + 2), F32)),
        in_specs=[anywhere] * 12,
        out_specs=(vmem, vmem),
        scratch_shapes=[
            S((2, LEAF), jnp.int32), S((FAR,), jnp.int32), S((FAR,), jnp.int32), S((COARSE,), jnp.int32), S((COARSE,), jnp.int32),
            S((FAR + COARSE,), jnp.int32), S((FAR,), jnp.int32),
            V((KRY, LEAF, PANEL), F32),
            V((LEAF, PANEL), F32),
            V((LEAF, RANK, PANEL), BF16),
            V((4, RANK, PANEL), BF16),
            V((LEAF, RANK, RANK), F32),
            V((LEAF, 2, PANEL, PANEL), BF16),
            V((FAR, RANK, RANK), F32),
            V((COARSE, RANK, RANK), F32),
            V((2, 4 * RANK, PANEL), BF16),
            V((5, 2, 4 * RANK, 4 * RANK), BF16),
            V((2, 4 * RANK, 4 * RANK), BF16),
            V((4 * LEAF, 4 * RANK), F32),
            V((LEAF, 2 * FAR), BF16),
            V((2, 40, 128), jnp.int32),
            V((64, 128), F32),
            V((2, 3, 128), F32),
            V((NROW, 3, 128), F32),
            V((NROW, 3, 128), F32),
            V((LEAF, PANEL), BF16),
            V((2, LEAF, PANEL), BF16),
            V((3 * LEAF, 2 * KRY, PANEL), BF16),
            V((3 * LEAF, PANEL), F32),
            V((3 * LEAF, PANEL), F32),
            V((KRY, LEAF, PANEL), F32),
            V((QROWS, 128), F32),
            V((NCORE, NROW // NCORE, 24, 128), F32),
            V((2, 40, KRY, 128), F32),
            V((KRY, 2, 40, 128), F32),
            V((2, 40, 128), F32),
            V((LEAF, PANEL), F32),
            V((LEAF, PANEL), BF16),
            V((NCOL, LEAF, PANEL), F32),
            V((NCOL, LEAF, PANEL), BF16),
            V((2, 8, 128), F32),
            V((2, NCOL, 8, 128), F32),
            V((1, 128), F32),
            V((NROW, 1, 128), F32),
            DMA((16,)),
            DMA((2,)), DMA((2,)),
            DMA((2, 2)), DMA((2, 2)),
            DMA((2,)), DMA((2,)),
            DMA((2,)), DMA((2,)),
            DMA(()), DMA(()),
            DMA(()), DMA(()), DMA(()), DMA(()), DMA((2,)), DMA((2,)),
        ],
        compiler_params=pltpu.CompilerParams(
            collective_id=0, has_side_effects=True, vmem_limit_bytes=60 * 2**20
        ),
        name="hmatrix_gmres",
    )(
        krylov,
        self_weight,
        cluster_basis,
        transfer,
        near_blocks,
        far_mat.reshape(FAR, RANK, RANK),
        coarse_mat.reshape(COARSE, RANK, RANK),
        near_cols.T,
        far_row.reshape(FAR),
        far_col.reshape(FAR),
        coarse_row.reshape(COARSE),
        coarse_col.reshape(COARSE),
    )
    return pl.pallas_call(
        copy_out,
        out_shape=shapes,
        in_specs=[vmem] * 2,
        out_specs=(anywhere, anywhere),
        scratch_shapes=[DMA((2,))],
        name="results",
    )(pltpu.with_memory_space_constraint(vectors, V), pltpu.with_memory_space_constraint(hessen, V))


def solution(mesh):
    in_specs = (
        P(None, "row", None),
        P("row", None),
        P("row", None, None),
        P("row", None, None),
        P("row", "col", None, None),
        P("row", "col"),
        P("row", "col", None),
        P("row", "col", None),
        P("row", "col", None, None, None),
        P("row", "col", None),
        P("row", "col", None),
        P("row", "col", None, None, None),
    )
    out_specs = (P(None, "row", None), P())
    return jax.shard_map(shards, mesh=mesh, in_specs=in_specs, out_specs=out_specs, check_vma=False)
```

```python
import functools

import jax
import jax.numpy as jnp
from jax import lax
from jax.experimental import pallas as pl
from jax.experimental.pallas import tpu as pltpu
from jax.sharding import PartitionSpec as P

MESH = pl.DeviceIdType.MESH
F32 = jnp.float32
BF16 = jnp.bfloat16

NX, NZ, NCORE, NCOL = 4, 8, 2, 4
NROW = NX * NZ * NCORE
LEAF, PANEL, RANK, KRY = 16, 256, 64, 8
LEAVES = NROW * LEAF
FAR, COARSE = 64, 16
QROWS = 21
COUNT = float(LEAVES * PANEL)


def iota(shape, dim):
    return lax.broadcasted_iota(jnp.int32, shape, dim)


def nt(a, b):
    return lax.dot_general(a, b, (((1,), (1,)), ((), ())), preferred_element_type=F32)


def split(x):
    hi = x.astype(BF16)
    return hi, (x - hi.astype(F32)).astype(BF16)


def fold(x):
    s = x[:, :128] + x[:, 128:]
    return s + pltpu.roll(s, 64, 1)


def partial_sum(x):
    s = x[:8] + x[8:]
    return jnp.sum(s[:, :128] + s[:, 128:], axis=0, keepdims=True)


def lanes_of(rows, first):
    sums = jnp.sum(rows, axis=1, keepdims=True)
    n = rows.shape[0]
    return jnp.sum(jnp.where(iota((n, 128), 1) == iota((n, 128), 0) + first, sums, 0.0), axis=0, keepdims=True)


def totals(pairs):
    eights = []
    for x, _ in pairs:
        s = x[:8] + x[8:]
        eights.append(s[:, :128] + s[:, 128:])
    sums = jnp.sum(jnp.concatenate(eights, axis=0), axis=1, keepdims=True)
    lane = iota((8, 128), 1)
    out = jnp.zeros((8, 128), F32)
    for j, (_, at) in enumerate(pairs):
        out = jnp.where(lane == at, sums[8 * j : 8 * j + 8], out)
    return jnp.sum(out, axis=0, keepdims=True)


def tree(x):
    n = x.shape[0]
    while n > 1:
        n //= 2
        x = x[:n] + x[n:]
    return x[0]


def kernel(
    kry_h, sw_h, cb_h, tr_h, nb_h, fm_h, cm_h, nc_h, fr_h, fc_h, cr_h, cc_h,
    out_v, out_h,
    nc_s, fr_s, fc_s, cr_s, cc_s, row_s, half_s,
    kry, sw, cb, bfar, tr, nb, fm, cm,
    pb, ftile, ttile, fmask, adds_to, fpar, gram_rows,
    pay, tab_a, tab_b, halo_src, halo, vq, vpad_a, vpad_b, nq, qpay, qtab, qgrow, qrows, grow, near_src_a, near_src_b, near_tab_a, near_tab_b, far_src, far_tab, sc_src, sc_tab,
    load_sem, pay_s, pay_r, halo_s, halo_r, near_s, near_r, far_s, far_r, sc_s, sc_r, q_s, q_r, qf_s, qf_r, vq_s, vq_r,
):
    tab, vpad = (tab_a, tab_b), (vpad_a, vpad_b)
    me = lax.axis_index("row")
    col = lax.axis_index("col")
    x = me // (NZ * NCORE)
    z = lax.rem(me // NCORE, NZ)
    core = lax.rem(me, NCORE)
    start = me * LEAF

    bar = pltpu.get_barrier_semaphore()

    def far_peer(k):
        jz = k // (NX * NCORE)
        rest = lax.rem(k, NX * NCORE)
        jx = rest // NCORE
        jc = lax.rem(rest, NCORE)
        dz = NZ // 2 + (1 - 2 * lax.rem(jz, 2)) * ((jz + 1) // 2) + NZ
        dx = NX // 2 + (1 - 2 * lax.rem(jx, 2)) * ((jx + 1) // 2) + NX
        pz = lax.rem(z + dz, NZ)
        px = lax.rem(x + dx, NX)
        pc = lax.rem(core + 1 + jc, NCORE)
        return (px * NZ + pz) * NCORE + pc

    def to_row(body):
        def step(k, c):
            body(far_peer(k))
            return c
        lax.fori_loop(0, NROW - 1, step, 0, unroll=7)

    to_row(lambda p: pl.semaphore_signal(bar, inc=1, device_id=(p, col), device_id_type=MESH))
    for k in range(1, NCOL):
        pl.semaphore_signal(bar, inc=1, device_id=(me, lax.rem(col + k, NCOL)), device_id_type=MESH)

    loads = []

    def load(src, dst):
        c = pltpu.make_async_copy(src, dst, load_sem.at[len(loads)])
        c.start()
        loads.append(c)
        return c

    l_kry = load(kry_h, kry)
    l_cb = load(cb_h, cb)
    l_bf = [load(cb_h.at[4 * k + col], bfar.at[k]) for k in range(4)]
    l_tr = load(tr_h, tr)
    def remote(src, dst, ssem, rsem, dev):
        pltpu.make_async_remote_copy(
            src_ref=src, dst_ref=dst, send_sem=ssem, recv_sem=rsem, device_id=dev, device_id_type=MESH
        ).start()

    def wait(ref, sem):
        pltpu.make_async_copy(ref, ref, sem).wait()

    lane256 = iota((LEAF, PANEL), 1) // RANK
    row256 = iota((LEAF, PANEL), 0)

    l_kry.wait()
    l_cb.wait()
    l_tr.wait()
    for k in range(4):
        child = 4 * col + k
        terms = jnp.concatenate(split(tr[child].T), axis=0)
        prod = jnp.dot(terms, cb[child], preferred_element_type=F32)
        hi, lo = split(prod[:RANK] + prod[RANK:])
        pb[0, RANK * k : RANK * (k + 1), :] = hi
        pb[1, RANK * k : RANK * (k + 1), :] = lo
    for c in l_bf:
        c.wait()
    l_index = [load(h, s) for h, s in ((nc_h, nc_s), (fr_h, fr_s), (fc_h, fc_s), (cr_h, cr_s), (cc_h, cc_s))]
    l_fm = load(fm_h, fm)
    l_cm = load(cm_h, cm)
    l_nb = load(nb_h, nb)
    l_sw = load(sw_h, sw)

    far_pick = (row256 == 4 * lane256 + col).astype(F32)
    par_pick = (row256 == 4 * col + lane256).astype(F32)

    def coefficients(hi, lo):
        n = hi.shape[0] // LEAF
        far = bfar[...].reshape(4 * RANK, PANEL)
        a, b = nt(hi, far), nt(hi, pb[0]) + nt(hi, pb[1])
        if lo is not None:
            a, b = a + nt(lo, far), b + nt(lo, pb[0])
        a = jnp.sum(a.reshape(n, LEAF, PANEL) * far_pick[None], axis=1)
        b = jnp.sum(b.reshape(n, LEAF, PANEL) * par_pick[None], axis=1)
        return a, fold(b)

    low1 = iota((1, 128), 1) < RANK

    def set_pay(step, hi, lo, extra):
        a, p = coefficients(hi, lo)
        pay[step, 0:1, :] = a[:, :128]
        pay[step, 1:2, :] = a[:, 128:]
        pay[step, 2:3, :] = jnp.where(low1, p, extra)

    last_hi = kry[KRY - 1].astype(BF16)
    set_pay(0, last_hi, None, jnp.zeros((1, 128), F32))
    halo_src[...] = last_hi
    vpad[0][LEAF : 2 * LEAF, :] = last_hi.astype(F32)
    for i in range(LEAF):
        hi, lo = split(kry[:, i, :])
        vq[LEAF + i] = jnp.concatenate([hi, lo], axis=0)

    pl.semaphore_wait(bar, NROW - 1 + NCOL - 1)

    up = lax.rem(me + 1, NROW)
    down = lax.rem(me + NROW - 1, NROW)

    def send_pay(step):
        tab[step][me] = pay[step]
        to_row(lambda p: remote(pay.at[step], tab[step].at[me], pay_s.at[step], pay_r.at[step], (p, col)))

    def to_neighbours(src, low, high, ssem, rsem):
        remote(src, low, ssem.at[0], rsem.at[0], (up, col))
        remote(src, high, ssem.at[1], rsem.at[1], (down, col))

    to_neighbours(halo_src, halo.at[0], halo.at[1], halo_s.at[0], halo_r.at[0])
    send_pay(0)

    for k in range(KRY):
        for l in range(k, KRY):
            r = partial_sum(kry[k] * kry[l])
            gram_rows[8 * k + l : 8 * k + l + 1, :] = r
            if l > k:
                gram_rows[8 * l + k : 8 * l + k + 1, :] = r
    chip = me // NCORE
    hi, lo = split(kry[...].reshape(KRY * LEAF, PANEL))
    a, p = coefficients(hi, lo)
    qpay[0:KRY, :] = a[:, :128]
    qpay[KRY : 2 * KRY, :] = a[:, 128:]
    qpay[QROWS - 1 :, :] = lanes_of(gram_rows[...], 64)
    qpay[2 * KRY : QROWS - 1, :] = jnp.where(iota((4, 128), 1) < RANK, p[:4], p[4:])
    qtab[core, chip, 0:QROWS, :] = qpay[...]

    def to_chip(k, c):
        peer = far_peer(NCORE * k) // NCORE * NCORE + core
        remote(qpay, qtab.at[core, chip, pl.ds(0, QROWS)], q_s, q_r, (peer, col))
        return c

    lax.fori_loop(0, NROW // NCORE - 1, to_chip, 0, unroll=4)
    l_fm.wait()
    l_cm.wait()
    for c in l_index:
        c.wait()
    for t in range(5):
        for n in range(4):
            if t < 4:
                four = [fm[16 * t + 4 * n + k] for k in range(4)]
            else:
                four = [cm[4 * n + k] for k in range(4)]
            hi, lo = split(jnp.concatenate(four, axis=1))
            ftile[t, 0, RANK * n : RANK * (n + 1), :] = hi
            ftile[t, 1, RANK * n : RANK * (n + 1), :] = lo
    for j in range(4):
        hi, lo = split(jnp.concatenate([tr[4 * g + j] for g in range(4)], axis=1))
        ttile[0, RANK * j : RANK * (j + 1), :] = hi
        ttile[1, RANK * j : RANK * (j + 1), :] = lo

    for n in range(4):
        row = jnp.zeros((LEAF, PANEL), jnp.int32)
        for k in range(4):
            row = jnp.where(lane256 == k, cr_s[4 * n + k] - 4 * me, row)
        fmask[LEAF * n : LEAF * (n + 1), :] = (row == row256 // 4).astype(F32)
    at = iota((LEAF, FAR), 1)
    row = jnp.zeros((LEAF, FAR), jnp.int32)
    for t in range(4):
        for odd in range(2):
            for n in range(4):
                for pair in range(2):
                    row = jnp.where(at == 16 * t + 8 * odd + 2 * n + pair, fr_s[16 * t + 4 * n + 2 * pair + odd] - start, row)
    adds = (row == iota((LEAF, FAR), 0)).astype(F32)
    adds_to[...] = jnp.concatenate([adds, adds], axis=1).astype(BF16)
    for b in range(FAR):
        within = lax.rem(fc_s[b], LEAF)
        row_s[b] = fc_s[b] // LEAF
        half_s[b] = within // 8
        half = lax.rem(within // 4, 2)
        fpar[b % 2, b // 2 : b // 2 + 1, :] = jnp.full((1, 128), half, jnp.int32)
    for b in range(COARSE):
        row_s[FAR + b] = cc_s[b] // 4
        fpar[b % 2, 32 + b // 2 : 33 + b // 2, :] = jnp.zeros((1, 128), jnp.int32)

    diag = (iota((RANK, PANEL), 0) // LEAF == iota((RANK, PANEL), 1) // RANK).astype(F32)

    def near_at(s, i):
        return jnp.minimum(lax.rem(nc_s[s, i] - start + LEAF + LEAVES, LEAVES), 3 * LEAF - 1)

    near_src, near_tab = (near_src_a, near_src_b), (near_tab_a, near_tab_b)

    def send_near(step, near):
        src, held = near_src[step], near_tab[step]
        src[...] = near.astype(src.dtype)
        held[col] = src[...]
        for k in range(1, NCOL):
            remote(src, held.at[col], near_s.at[step], near_r.at[step], (me, lax.rem(col + k, NCOL)))

    def near_last():
        def body(i, acc):
            out = jnp.zeros((LEAF, PANEL), F32)
            for s in range(2):
                v = jnp.broadcast_to(vpad[0][pl.ds(near_at(s, i), 1), :], (LEAF, PANEL))
                out = out + nt(v.astype(BF16), nb[i, s])
            return jnp.where(row256 == i, out, acc)

        return lax.fori_loop(0, LEAF, body, jnp.zeros((LEAF, PANEL), F32), unroll=16)

    def near_new():
        def body(i, acc):
            out = jnp.zeros((2 * LEAF, PANEL), F32)
            for s in range(2):
                at = near_at(s, i)
                v = jnp.broadcast_to(vpad[1][pl.ds(at, 1), :], (LEAF, PANEL))
                lhs = jnp.where(row256 < 8, v, v - v.astype(BF16).astype(F32)).astype(BF16)
                out = out + nt(jnp.concatenate([vq[at], lhs], axis=0), nb[i, s])
            nq[:, pl.ds(i, 1), :] = (out[0:8] + out[8:16]).reshape(KRY, 1, PANEL)
            return jnp.where(row256 == i, out[16:17] + out[24:25], acc)

        return lax.fori_loop(0, LEAF, body, jnp.zeros((LEAF, PANEL), F32), unroll=16)

    def product(t, rows, first):
        xs = []
        for n in range(4):
            r = jnp.concatenate([rows[first + 2 * n : first + 2 * n + 1], rows[first + 2 * n + 1 : first + 2 * n + 2]], axis=1)
            xs.append(jnp.broadcast_to(r, (LEAF, PANEL)))
        hi, lo = split(jnp.concatenate(xs, axis=0) * fmask[...])
        o = nt(jnp.concatenate([hi, lo], axis=0), ftile[t, 0])
        return o[:RANK] + o[RANK:] + nt(hi, ftile[t, 1])

    row16, lane128 = iota((LEAF, 128), 0), iota((LEAF, 128), 1)
    own_half = ((row16 // 8) == (lane128 // RANK)).astype(F32)
    own_pair = [own_half * (lax.rem(row16, 2) == j).astype(F32) for j in range(2)]
    own_group = (lax.rem(row256, 8) // 2 == lane256).astype(F32)

    def block_results(t, rows):
        both = jnp.concatenate([rows, rows], axis=0)
        hi, lo = split(jnp.concatenate([both * own_pair[0], both * own_pair[1]], axis=1))
        o = nt(jnp.concatenate([hi, lo], axis=0), ftile[t, 0])
        return fold((o[:LEAF] + o[LEAF:] + nt(hi, ftile[t, 1])) * own_group)

    def over_groups(o):
        o = o * diag
        return (o[0:16] + o[16:32]) + (o[32:48] + o[48:64])

    def halves(even, odd):
        return jnp.where(
            iota((40, 128), 1) < RANK,
            jnp.where(fpar[0] == 0, even, pltpu.roll(even, 64, 1)),
            jnp.where(fpar[1] == 1, odd, pltpu.roll(odd, 64, 1)),
        )

    def gather(step):
        for b in range(FAR):
            grow[b % 2, b // 2 : b // 2 + 1, :] = tab[step][row_s[b], pl.ds(half_s[b], 1), :]
        for b in range(COARSE):
            grow[b % 2, 32 + b // 2 : 33 + b // 2, :] = tab[step][row_s[FAR + b], 2:3, :]
        return grow[0], grow[1]

    def gather_given():
        for b in range(FAR):
            r = row_s[b]
            second = jnp.full((KRY, 128), half_s[b], jnp.int32) == 1
            both = qtab[lax.rem(r, NCORE), r // NCORE, 0 : 2 * KRY, :]
            qgrow[b % 2, b // 2] = jnp.where(second, both[KRY:], both[:KRY])
        for b in range(COARSE):
            r = row_s[FAR + b]
            pair = qtab[lax.rem(r, NCORE), r // NCORE, 2 * KRY : QROWS - 1, :]
            turned = pltpu.roll(pair, 64, 1)
            low = iota((4, 128), 1) < RANK
            qgrow[b % 2, 32 + b // 2, 0:4, :] = jnp.where(low, pair, turned)
            qgrow[b % 2, 32 + b // 2, 4:8, :] = jnp.where(low, turned, pair)
        for k in range(KRY):
            for p in range(2):
                qrows[k, p] = qgrow[p, :, k, :]

    def far_part(step, even, odd):
        rows = halves(even, odd)
        cres = fold(over_groups(product(4, rows, 32)))
        blocks = jnp.concatenate([block_results(t, rows[8 * t : 8 * t + 8]) for t in range(4)], axis=0)
        far = jnp.dot(adds_to[...], jnp.concatenate(split(blocks), axis=0), preferred_element_type=F32)
        hi, lo = split(jnp.concatenate([cres, cres], axis=1) * (lane256 == row256 // 4).astype(F32))
        o = nt(jnp.concatenate([hi, lo], axis=0), ttile[0])
        down = o[:LEAF] + o[LEAF:] + nt(hi, ttile[1])
        total = far + fold(down * (lane256 == lax.rem(row256, 4)).astype(F32))
        far_src[step] = jnp.where(iota((8, 128), 1) < RANK, total[:8], total[8:])
        far_tab[step, col] = far_src[step]
        for k in range(1, NCOL):
            remote(far_src.at[step], far_tab.at[step, col], far_s.at[step], far_r.at[step], (me, lax.rem(col + k, NCOL)))

    back_mask = jnp.concatenate([(row256 == 4 * g + lane256).astype(F32) for g in range(4)], axis=1)

    def assemble(step, v, scale):
        wait(near_tab[step].at[pl.ds(0, NCOL - 1)], near_r.at[step])
        parts = [near_tab[step][c].astype(F32) for c in range(NCOL)]
        near = (parts[0] + parts[1]) + (parts[2] + parts[3])
        if scale is not None:
            near = near * scale
        base = sw[...] * v + near
        wait(far_tab.at[step, pl.ds(0, NCOL - 1)], far_r.at[step])
        far = (far_tab[step, 0] + far_tab[step, 1]) + (far_tab[step, 2] + far_tab[step, 3])
        if scale is not None:
            far = far * scale
        back = pltpu.roll(far, 64, 1)
        low = iota((8, 128), 1) < RANK
        both = jnp.concatenate([jnp.where(low, far, back), jnp.where(low, back, far)], axis=0)
        lhs = (jnp.concatenate([both] * 8, axis=1) * back_mask).astype(BF16)
        return base + jnp.dot(lhs, cb[...].reshape(LEAF * RANK, PANEL), preferred_element_type=F32)

    def exchange(row):
        sc_src[...] = row
        sc_tab[me] = row
        to_row(lambda p: remote(sc_src, sc_tab.at[me], sc_s, sc_r, (p, col)))

    lane1 = iota((1, 128), 1)
    sq = (iota((8, 128), 0) == iota((8, 128), 1))

    def pick(row, k):
        return row[:, k : k + 1]

    l_nb.wait()
    for j in range(2):
        wait(halo.at[j], halo_r.at[0, j])
        vpad[0][2 * LEAF * j : 2 * LEAF * j + LEAF, :] = halo[j].astype(F32)
    send_near(0, near_last())
    own = vq.at[pl.ds(LEAF, LEAF)]
    to_neighbours(own, vq.at[pl.ds(0, LEAF)], vq.at[pl.ds(2 * LEAF, LEAF)], vq_s, vq_r)

    wait(tab[0].at[pl.ds(0, NROW - 1)], pay_r.at[0])
    far_part(0, *gather(0))
    l_sw.wait()
    w = assemble(0, kry[KRY - 1], None)

    def quadratic(tot):
        gh = jnp.sum(gram * tot, axis=1, keepdims=True)
        hcol = jnp.sum(jnp.where(sq, tot, 0.0), axis=1, keepdims=True)
        return jnp.sum(gh * hcol, axis=0, keepdims=True)

    vpad[1][LEAF : 2 * LEAF, :] = w
    own = vpad[1].at[pl.ds(LEAF, LEAF)]
    to_neighbours(own, vpad[1].at[pl.ds(0, LEAF)], vpad[1].at[pl.ds(2 * LEAF, LEAF)], halo_s.at[1], halo_r.at[1])
    hi, lo = split(w)
    set_pay(1, hi, lo, totals([(kry[k] * w, RANK + k) for k in range(KRY)] + [(w * w, RANK + KRY)]))
    send_pay(1)

    some = qtab.at[core, pl.ds(0, NROW // NCORE - 1), pl.ds(0, QROWS)]
    half = qtab.at[core, :, pl.ds(0, QROWS)]
    wait(some, q_r)
    remote(half, half, qf_s, qf_r, (me + 1 - 2 * core, col))
    for j in range(2):
        wait(vpad[1].at[pl.ds(2 * LEAF * j, LEAF)], halo_r.at[1, j])
        wait(vq.at[pl.ds(2 * LEAF * j, LEAF)], vq_r.at[j])
    near = near_new()
    wait(half, qf_r)
    gather_given()
    gsum = jnp.sum(qtab[:, :, QROWS - 1 : QROWS, :].reshape(NROW, 1, 128), axis=0) * (1.0 / COUNT)
    gram = jnp.zeros((8, 128), F32)
    for k in range(KRY):
        gram = jnp.where(iota((8, 128), 0) == k, pltpu.roll(gsum, 64 - 8 * k, 1), gram)
    gram = jnp.where(iota((8, 128), 1) < KRY, gram, 0.0)

    wait(tab[1].at[pl.ds(0, NROW - 1)], pay_r.at[1])
    tot = pltpu.roll(tree(tab[1][...])[2:3], 64, 1) * (1.0 / COUNT)
    h_row = jnp.where(lane1 < KRY, tot, 0.0)
    hh = jnp.sum(h_row * h_row, axis=1, keepdims=True)
    norm = pick(tot, KRY) - 2.0 * hh + quadratic(h_row)
    beta = jnp.sqrt(jnp.maximum(norm, 0.0) + 1e-06)
    inv = 1.0 / beta
    hs = [pick(tot, k) for k in range(KRY)]

    def less(v, of):
        for k in range(KRY):
            v = v - hs[k] * of[k]
        return v

    send_near(1, less(near, nq))
    far_part(1, *[less(g, qrows.at[:, p]) for p, g in enumerate(gather(1))])
    q = less(w, kry) * inv
    out_v[0] = q
    line = jnp.where(lane1 == KRY + 1, beta, h_row)
    out_h[0:1, :] = line[:, : KRY + 2]
    new_gram = totals([(kry[k] * q, 16 + k) for k in range(KRY)] + [(q * q, 16 + KRY)])
    w = assemble(1, q, inv)
    exchange(new_gram + totals([(kry[k] * w, k) for k in range(KRY)] + [(q * w, KRY), (w * w, KRY + 1)]))
    wait(sc_tab.at[pl.ds(0, NROW - 1)], sc_r)
    tot = tree(sc_tab[...]) * (1.0 / COUNT)
    h_all = jnp.where(lane1 <= KRY, tot, 0.0)
    h_row = jnp.where(lane1 < KRY, tot, 0.0)
    g_row = jnp.where(lane1 <= KRY, pltpu.roll(tot, 128 - 16, 1), 0.0)
    hh = jnp.sum(h_all * h_all, axis=1, keepdims=True)
    hg = jnp.sum(h_all * g_row, axis=1, keepdims=True)
    h8 = pick(tot, KRY)
    norm = pick(tot, KRY + 1) - 2.0 * hh + quadratic(h_row) + 2.0 * h8 * hg - h8 * h8 * pick(g_row, KRY)
    beta = jnp.sqrt(jnp.maximum(norm, 0.0) + 1e-06)
    w2 = w - h8 * q
    for k in range(KRY):
        w2 = w2 - pick(tot, k) * kry[k]
    out_v[1] = w2 * (1.0 / beta)
    line = jnp.where(lane1 == KRY + 1, beta, h_all)
    out_h[1:2, :] = line[:, : KRY + 2]

    for step in range(2):
        wait(tab[step].at[pl.ds(0, NROW - 1)], pay_s.at[step])
        wait(near_tab[step].at[pl.ds(0, NCOL - 1)], near_s.at[step])
        wait(far_tab.at[step, pl.ds(0, NCOL - 1)], far_s.at[step])
    for j in range(2):
        wait(halo.at[j], halo_s.at[0, j])
        wait(vpad[1].at[pl.ds(LEAF, LEAF)], halo_s.at[1, j])
        wait(vq.at[pl.ds(LEAF, LEAF)], vq_s.at[j])
    wait(sc_tab.at[pl.ds(0, NROW - 1)], sc_s)
    wait(some, q_s)
    wait(half, qf_s)


def copy_out(v_in, h_in, v_out, h_out, sem):
    copies = [pltpu.make_async_copy(v_in, v_out, sem.at[0]), pltpu.make_async_copy(h_in, h_out, sem.at[1])]
    for c in copies:
        c.start()
    for c in copies:
        c.wait()


def shards(krylov, self_weight, cluster_basis, transfer, near_blocks, near_cols, far_row, far_col, far_mat, coarse_row, coarse_col, coarse_mat):
    anywhere = pl.BlockSpec(memory_space=pl.ANY)
    S = pltpu.SMEM
    vmem = pl.BlockSpec(memory_space=pltpu.VMEM)
    V = pltpu.VMEM
    DMA = pltpu.SemaphoreType.DMA
    shapes = (jax.ShapeDtypeStruct((2, LEAF, PANEL), F32), jax.ShapeDtypeStruct((2, KRY + 2), F32))
    vectors, hessen = pl.pallas_call(
        kernel,
        out_shape=(V((2, LEAF, PANEL), F32), V((2, KRY + 2), F32)),
        in_specs=[anywhere] * 12,
        out_specs=(vmem, vmem),
        scratch_shapes=[
            S((2, LEAF), jnp.int32), S((FAR,), jnp.int32), S((FAR,), jnp.int32), S((COARSE,), jnp.int32), S((COARSE,), jnp.int32),
            S((FAR + COARSE,), jnp.int32), S((FAR,), jnp.int32),
            V((KRY, LEAF, PANEL), F32),
            V((LEAF, PANEL), F32),
            V((LEAF, RANK, PANEL), BF16),
            V((4, RANK, PANEL), BF16),
            V((LEAF, RANK, RANK), F32),
            V((LEAF, 2, PANEL, PANEL), BF16),
            V((FAR, RANK, RANK), F32),
            V((COARSE, RANK, RANK), F32),
            V((2, 4 * RANK, PANEL), BF16),
            V((5, 2, 4 * RANK, 4 * RANK), BF16),
            V((2, 4 * RANK, 4 * RANK), BF16),
            V((4 * LEAF, 4 * RANK), F32),
            V((LEAF, 2 * FAR), BF16),
            V((2, 40, 128), jnp.int32),
            V((64, 128), F32),
            V((2, 3, 128), F32),
            V((NROW, 3, 128), F32),
            V((NROW, 3, 128), F32),
            V((LEAF, PANEL), BF16),
            V((2, LEAF, PANEL), BF16),
            V((3 * LEAF, 2 * KRY, PANEL), BF16),
            V((3 * LEAF, PANEL), F32),
            V((3 * LEAF, PANEL), F32),
            V((KRY, LEAF, PANEL), F32),
            V((QROWS, 128), F32),
            V((NCORE, NROW // NCORE, 24, 128), F32),
            V((2, 40, KRY, 128), F32),
            V((KRY, 2, 40, 128), F32),
            V((2, 40, 128), F32),
            V((LEAF, PANEL), F32),
            V((LEAF, PANEL), BF16),
            V((NCOL, LEAF, PANEL), F32),
            V((NCOL, LEAF, PANEL), BF16),
            V((2, 8, 128), F32),
            V((2, NCOL, 8, 128), F32),
            V((1, 128), F32),
            V((NROW, 1, 128), F32),
            DMA((16,)),
            DMA((2,)), DMA((2,)),
            DMA((2, 2)), DMA((2, 2)),
            DMA((2,)), DMA((2,)),
            DMA((2,)), DMA((2,)),
            DMA(()), DMA(()),
            DMA(()), DMA(()), DMA(()), DMA(()), DMA((2,)), DMA((2,)),
        ],
        compiler_params=pltpu.CompilerParams(
            collective_id=0, has_side_effects=True, vmem_limit_bytes=60 * 2**20
        ),
        name="hmatrix_gmres",
    )(
        krylov,
        self_weight,
        cluster_basis,
        transfer,
        near_blocks,
        far_mat.reshape(FAR, RANK, RANK),
        coarse_mat.reshape(COARSE, RANK, RANK),
        near_cols.T,
        far_row.reshape(FAR),
        far_col.reshape(FAR),
        coarse_row.reshape(COARSE),
        coarse_col.reshape(COARSE),
    )
    return pl.pallas_call(
        copy_out,
        out_shape=shapes,
        in_specs=[vmem] * 2,
        out_specs=(anywhere, anywhere),
        scratch_shapes=[DMA((2,))],
        name="results",
    )(pltpu.with_memory_space_constraint(vectors, V), pltpu.with_memory_space_constraint(hessen, V))


def solution(mesh):
    in_specs = (
        P(None, "row", None),
        P("row", None),
        P("row", None, None),
        P("row", None, None),
        P("row", "col", None, None),
        P("row", "col"),
        P("row", "col", None),
        P("row", "col", None),
        P("row", "col", None, None, None),
        P("row", "col", None),
        P("row", "col", None),
        P("row", "col", None, None, None),
    )
    out_specs = (P(None, "row", None), P())
    return jax.shard_map(shards, mesh=mesh, in_specs=in_specs, out_specs=out_specs, check_vma=False)
```
